256 devices in a mesh: mic: 4 (over y_lo, core), tm: 64 (over y_hi, z, x).
Axes of the slice: x: 4, y: 4 (y_hi: 2, y_lo: 2; y = y_hi * 2 + y_lo), z: 8, core: 2. Of those that a mesh axis runs over, the one named last changes fastest.
Arguments:
- frames: bfloat16 [8, 8192, 512], P('mic', 'tm'), may hold values from -6 to 6
- cotangent: bfloat16 [8, 8192, 512], P('mic', 'tm'), may hold values from -6 to 6
- kernel: float32 [31, 512], replicated, may hold values from -1 to 1
- w_query: bfloat16 [512, 512], replicated, may hold values from -0.25 to 0.25
- w_key: bfloat16 [512, 512], replicated, may hold values from -0.25 to 0.25
- w_value: bfloat16 [512, 512], replicated, may hold values from -0.25 to 0.25
- w_out: bfloat16 [512, 512], replicated, may hold values from -0.25 to 0.25
Outputs:
- layer_out: bfloat16 [8, 8192, 512], P('mic', 'tm')
- frame_grad: bfloat16 [8, 8192, 512], P('mic', 'tm')
- kernel_grad: float32 [31, 512], replicated
- query_grad: float32 [512, 512], replicated
- key_grad: float32 [512, 512], replicated
- value_grad: float32 [512, 512], replicated
- out_grad: float32 [512, 512], replicated
The draws below stay inside these ranges and needn't reach their ends.
All inputs are finite; a program needn't handle non-finite values.
Results may differ from the reference program's by a relative error of at most 0.013.
Values may be sent and summed in bfloat16 or wider, within the bound.
A program may use at most 128 MiB of HBM per device.

```python
import math
import jax
import jax.numpy as jnp
from jax import lax

D = 512
HEADS = 8
KERNEL = 31
MICS = 8
TIME = 8192


def block_scale(rng, shape, cuts, low, largest):
    level, own = 1.0, jax.random.fold_in(rng, 6)
    for axis_at, blocks in cuts:
        heights = jnp.exp(jax.random.uniform(jax.random.fold_in(own, axis_at), (blocks,), jnp.float32, low / len(cuts), largest / len(cuts)))
        level = level * jnp.repeat(heights, shape[axis_at] // blocks).reshape([-1 if axis == axis_at else 1 for axis in range(len(shape))])
    return level


def gaussian(own_key, extent, scale, most, pieces=(), kind=jnp.bfloat16):
    level = block_scale(own_key, extent, pieces, -0.22, 0.18) if pieces else 1.0
    entries = jax.random.normal(own_key, extent, jnp.float32) * scale * level
    return jnp.minimum(jnp.maximum(entries, -most), most).astype(kind)


def setup_inputs(seed: int = 0) -> dict:
    key_of = jax.random.split(jax.random.key(seed), 8)
    return {
        "frames": gaussian(key_of[0], (MICS, TIME, D), 1.0, 6.0, ((0, 4), (1, 64))),
        "cotangent": gaussian(key_of[1], (MICS, TIME, D), 1.0, 6.0, ((0, 4), (1, 64))),
        "kernel": gaussian(key_of[2], (KERNEL, D), KERNEL ** -0.5, 1.0, (), jnp.float32),
        "w_query": gaussian(key_of[3], (D, D), D ** -0.5, 0.25),
        "w_key": gaussian(key_of[4], (D, D), D ** -0.5, 0.25),
        "w_value": gaussian(key_of[5], (D, D), D ** -0.5, 0.25),
        "w_out": gaussian(key_of[6], (D, D), D ** -0.5, 0.25),
    }


def depthwise(padded, kernel, length):
    summed = jnp.zeros((padded.shape[0], length, padded.shape[2]), jnp.float32)
    for offset in range(kernel.shape[0]):
        summed = summed + padded[:, offset:offset + length, :].astype(jnp.float32) * kernel[offset]
    return summed

def transposed(padded, kernel, length):
    reach = kernel.shape[0] - 1
    summed = jnp.zeros((padded.shape[0], length, padded.shape[2]), jnp.float32)
    for offset in range(kernel.shape[0]):
        start = reach - offset
        summed = summed + padded[:, start:start + length, :] * kernel[offset]
    return summed

def kernel_terms(padded, gradient, taps):
    length = gradient.shape[1]
    rows_out = []
    for offset in range(taps):
        rows_out.append(lax.optimization_barrier(jnp.sum(padded[:, offset:offset + length, :].astype(jnp.float32) * gradient, axis=(0, 1))))
    return jnp.stack(rows_out)

def attend(queries, key_rows, value_rows, head_count):
    first, length, width = queries.shape
    others = key_rows.shape[0]
    depth = width // head_count
    factor = 1.0 / math.sqrt(depth)
    query_heads = queries.astype(jnp.float32).reshape(first, length, head_count, depth)
    key_heads = key_rows.astype(jnp.float32).reshape(others, length, head_count, depth)
    value_heads = value_rows.astype(jnp.float32).reshape(others, length, head_count, depth)
    scores = jnp.einsum('athe,bthe->abth', query_heads, key_heads) * factor
    weights = jnp.exp(scores)
    weights = weights / lax.optimization_barrier(jnp.sum(weights, axis=1, keepdims=True))
    mixed = jnp.einsum('abth,bthe->athe', weights, value_heads).reshape(first, length, width)
    return (mixed, weights)

def attend_back(queries, key_rows, value_rows, weights, upstream, head_count):
    first, length, width = queries.shape
    others = key_rows.shape[0]
    depth = width // head_count
    factor = 1.0 / math.sqrt(depth)
    query_heads = queries.astype(jnp.float32).reshape(first, length, head_count, depth)
    key_heads = key_rows.astype(jnp.float32).reshape(others, length, head_count, depth)
    value_heads = value_rows.astype(jnp.float32).reshape(others, length, head_count, depth)
    up_heads = upstream.astype(jnp.float32).reshape(first, length, head_count, depth)
    products = jnp.einsum('athe,bthe->abth', up_heads, value_heads)
    inner = weights * (products - lax.optimization_barrier(jnp.sum(weights * products, axis=1, keepdims=True))) * factor
    dquery = jnp.einsum('abth,bthe->athe', inner, key_heads).reshape(first, length, width)
    key_terms = jnp.einsum('abth,athe->bthe', inner, query_heads).reshape(others, length, width)
    value_terms = jnp.einsum('abth,athe->bthe', weights, up_heads).reshape(others, length, width)
    return (dquery, key_terms, value_terms)

def project(inputs, matrix):
    width = inputs.shape[-1]
    return jnp.dot(inputs.reshape(-1, width), matrix, preferred_element_type=jnp.float32).reshape(inputs.shape[:-1] + (matrix.shape[1],))

def outer(left, right):
    width = left.shape[-1]
    return jnp.dot(left.reshape(-1, width).T, right.reshape(-1, right.shape[-1]), preferred_element_type=jnp.float32)

def reference(frames, cotangent, kernel, w_query, w_key, w_value, w_out):
    reach = kernel.shape[0] // 2
    length = frames.shape[1]
    padded = jnp.pad(frames, ((0, 0), (reach, reach), (0, 0)))
    conv = depthwise(padded, kernel, length)
    acted = jax.nn.silu(conv).astype(jnp.bfloat16)
    queries = project(acted, w_query).astype(jnp.bfloat16)
    key_rows = project(acted, w_key).astype(jnp.bfloat16)
    value_rows = project(acted, w_value).astype(jnp.bfloat16)
    mixed, weights = attend(queries, key_rows, value_rows, HEADS)
    mixed = mixed.astype(jnp.bfloat16)
    layer_out = (frames.astype(jnp.float32) + project(mixed, w_out)).astype(jnp.bfloat16)
    upstream = project(cotangent, w_out.T).astype(jnp.bfloat16)
    out_term = outer(mixed, cotangent)
    dquery, key_terms, value_terms = attend_back(queries, key_rows, value_rows, weights, upstream, HEADS)
    dquery = dquery.astype(jnp.bfloat16)
    dkey = key_terms.astype(jnp.bfloat16)
    dvalue = value_terms.astype(jnp.bfloat16)
    dacted = project(dquery, w_query.T) + project(dkey, w_key.T) + project(dvalue, w_value.T)
    sig = jax.nn.sigmoid(conv)
    dconv = dacted * sig * (1.0 + conv * (1.0 - sig))
    grad_pad = jnp.pad(dconv, ((0, 0), (reach, reach), (0, 0)))
    frame_grad = (cotangent.astype(jnp.float32) + transposed(grad_pad, kernel, length)).astype(jnp.bfloat16)
    norm_factor = 1.0 / math.sqrt(frames.shape[0] * frames.shape[1])
    kernel_grad = kernel_terms(padded, dconv, kernel.shape[0]) * norm_factor
    query_grad = outer(acted, dquery) * norm_factor
    key_grad = outer(acted, dkey) * norm_factor
    value_grad = outer(acted, dvalue) * norm_factor
    out_grad = out_term * norm_factor
    return (layer_out, frame_grad, kernel_grad, query_grad, key_grad, value_grad, out_grad)
```

```python
import functools
import math

import jax
import jax.numpy as jnp
from jax import lax
from jax.experimental import pallas as pl
from jax.experimental.pallas import tpu as pltpu
from jax.sharding import PartitionSpec as P

HEADS = 8
NX, NY, NZ = 4, 4, 8
MESH = pl.DeviceIdType.MESH


class Place:
    def __init__(self):
        mic = lax.axis_index("mic")
        tm = lax.axis_index("tm")
        self.core = lax.rem(mic, 2)
        self.x = lax.rem(tm, NX)
        self.z = lax.rem(lax.div(tm, NX), NZ)
        self.y = lax.div(tm, NX * NZ) * 2 + lax.div(mic, 2)

    def device(self, x=None, y=None, z=None, core=None):
        x = self.x if x is None else x
        y = self.y if y is None else y
        z = self.z if z is None else z
        core = self.core if core is None else core
        mic = lax.rem(y, 2) * 2 + core
        tm = lax.div(y, 2) * (NX * NZ) + z * NX + x
        return (mic, tm)

    def along(self, axis, step):
        size = {"x": NX, "y": NY, "z": NZ, "core": 2}[axis]
        index = lax.rem(getattr(self, axis) + step, size)
        return index, self.device(**{axis: index})


def rows_at(start, count):
    return pl.ds(pl.multiple_of(start, count), count)


def send(src, dst, send_sem, recv_sem, device):
    copy = pltpu.make_async_remote_copy(
        src_ref=src,
        dst_ref=dst,
        send_sem=send_sem,
        recv_sem=recv_sem,
        device_id=device,
        device_id_type=MESH,
    )
    copy.start()
    return copy


def greet(peers):
    barrier = pltpu.get_barrier_semaphore()
    for peer in peers:
        pl.semaphore_signal(barrier, inc=1, device_id=peer, device_id_type=MESH)
    pl.semaphore_wait(barrier, len(peers))


SIZES = {"x": NX, "y": NY, "z": NZ, "core": 2}
HALF, STREAM, FIRST, SECOND, TILE = 4096, 2048, 512, 128, 16
ORDERS = (("x", "y", "z"), ("y", "x", "z"))


def f32(value):
    return value.astype(jnp.float32)


def sum_kernel(
    scale,
    q_ref,
    k_ref,
    v_ref,
    o_ref,
    tap_ref,
    out_ref,
    tap_out,
    mine,
    full,
    core_rx,
    rx1,
    rx2,
    rx3,
    tap0,
    tap_zrx,
    tap_rx,
    tap_full,
    core_s,
    core_r,
    s1,
    r1,
    s2,
    r2,
    s3,
    r3,
    gs,
    gr,
    gcs,
    gcr,
    ts,
    tr,
    tgs,
    tgr,
):
    here = Place()
    peers = []
    for axis in ("core", "x", "y", "z"):
        for step in range(1, SIZES[axis]):
            peers.append(here.along(axis, step)[1])
    greet(peers)
    sent = []
    own = here.core * HALF
    other, sibling = here.along("core", 1)
    for g, ref in enumerate((q_ref, k_ref, v_ref, o_ref)):
        for block in range(4):
            at = (g * 4 + block) * 512
            mine[at : at + 512, :] = ref[:, block * 128 : (block + 1) * 128].astype(jnp.bfloat16)
    for s in range(2):
        sent.append(
            send(
                mine.at[rows_at(other * HALF + s * STREAM, STREAM)],
                core_rx.at[s],
                core_s.at[s],
                core_r.at[s],
                sibling,
            )
        )
    core_copies = sent[:]
    for block in range(4):
        tap0[block * 32 : block * 32 + 32, :] = tap_ref[:, block * 128 : (block + 1) * 128]
    tap_copies = []
    for step in range(1, NZ):
        index, peer = here.along("z", step)
        tap_copies.append(
            send(
                tap0.at[rows_at(index * 16, 16)],
                tap_zrx.at[step - 1],
                ts.at[step - 1],
                tr.at[step - 1],
                peer,
            )
        )
    sent += tap_copies

    first = []
    for s in range(2):
        core_copies[s].wait_recv()
        part = rows_at(own + s * STREAM, STREAM)
        mine[part, :] = (f32(mine[part, :]) + f32(core_rx[s])).astype(jnp.bfloat16)
        axis = ORDERS[s][0]
        copies = []
        for step in range(1, SIZES[axis]):
            index, peer = here.along(axis, step)
            copies.append(
                send(
                    mine.at[rows_at(own + s * STREAM + index * FIRST, FIRST)],
                    rx1.at[s, step - 1],
                    s1.at[s, step - 1],
                    r1.at[s, step - 1],
                    peer,
                )
            )
        first.append(copies)
        sent += copies

    total = tap0[rows_at(here.z * 16, 16), :]
    for step in range(1, NZ):
        tap_copies[step - 1].wait_recv()
        total = total + tap_zrx[step - 1]

    def tap_axis(tile, axis, base):
        slot = base + getattr(here, axis)
        tap_rx[slot] = tile
        copies = []
        for step in range(1, SIZES[axis]):
            copies.append(
                send(
                    tap_rx.at[slot],
                    tap_rx.at[slot],
                    ts.at[NZ - 1 + base + step - 1],
                    tr.at[NZ - 1 + base + step - 1],
                    here.along(axis, step)[1],
                )
            )
        return copies

    def tap_sum(copies, base):
        for copy in copies:
            copy.wait_recv()
        total = tap_rx[base]
        for index in range(len(copies)):
            total = total + tap_rx[base + 1 + index]
        return total

    tap_x = tap_axis(total, "x", 0)
    sent += tap_x

    second = []
    for s in range(2):
        axis, axis2, _ = ORDERS[s]
        place = own + s * STREAM + getattr(here, axis) * FIRST
        for copy in first[s]:
            copy.wait_recv()
        part = rows_at(place, FIRST)
        total = f32(mine[part, :])
        for step in range(SIZES[axis] - 1):
            total = total + f32(rx1[s, step])
        mine[part, :] = total.astype(jnp.bfloat16)
        copies = []
        for step in range(1, SIZES[axis2]):
            index, peer = here.along(axis2, step)
            copies.append(
                send(
                    mine.at[rows_at(place + index * SECOND, SECOND)],
                    rx2.at[s, step - 1],
                    s2.at[s, step - 1],
                    r2.at[s, step - 1],
                    peer,
                )
            )
        second.append((place, copies))
        sent += copies

    tap_y = tap_axis(tap_sum(tap_x, 0), "y", 4)
    sent += tap_y

    third = []
    for s in range(2):
        axis2 = ORDERS[s][1]
        place, copies = second[s]
        place = place + getattr(here, axis2) * SECOND
        for copy in copies:
            copy.wait_recv()
        part = rows_at(place, SECOND)
        total = f32(mine[part, :])
        for step in range(SIZES[axis2] - 1):
            total = total + f32(rx2[s, step])
        mine[part, :] = total.astype(jnp.bfloat16)
        copies = []
        for step in range(1, NZ):
            index, peer = here.along("z", step)
            copies.append(
                send(
                    mine.at[rows_at(place + index * TILE, TILE)],
                    rx3.at[s, step - 1],
                    s3.at[s, step - 1],
                    r3.at[s, step - 1],
                    peer,
                )
            )
        third.append((place, copies))
        sent += copies

    tap_c = tap_axis(tap_sum(tap_y, 4), "core", 8)
    sent += tap_c

    def gather(s, level, axis, place, count):
        copies = []
        base = (0, NZ - 1, NZ + 2)[level]
        part = rows_at(place, count)
        for step in range(1, SIZES[axis]):
            copies.append(
                send(
                    full.at[part],
                    full.at[part],
                    gs.at[s, base + step - 1],
                    gr.at[s, base + step - 1],
                    here.along(axis, step)[1],
                )
            )
        return copies

    back = []
    for s in range(2):
        place, copies = third[s]
        for copy in copies:
            copy.wait_recv()
        part = rows_at(place + here.z * TILE, TILE)
        total = f32(mine[part, :])
        for step in range(NZ - 1):
            total = total + f32(rx3[s, step])
        full[part, :] = (total * scale).astype(jnp.bfloat16)
        copies = gather(s, 0, "z", place + here.z * TILE, TILE)
        back.append((place, copies))
        sent += copies

    part = rows_at(here.z * 16, 16)
    tap_full[part, :] = tap_sum(tap_c, 8) * scale
    tap_back = []
    for step in range(1, NZ):
        tap_back.append(
            send(
                tap_full.at[part],
                tap_full.at[part],
                tgs.at[step - 1],
                tgr.at[step - 1],
                here.along("z", step)[1],
            )
        )
    sent += tap_back

    for level in (1, 2):
        for s in range(2):
            place, copies = back[s]
            for copy in copies:
                copy.wait_recv()
            axis = ORDERS[s][2 - level]
            count = (TILE, SECOND, FIRST)[level]
            copies = gather(s, level, axis, place, count)
            back[s] = (place - getattr(here, axis) * count, copies)
            sent += copies
    last = []
    for s in range(2):
        place, copies = back[s]
        for copy in copies:
            copy.wait_recv()
        part = rows_at(own + s * STREAM, STREAM)
        copy = send(full.at[part], full.at[part], gcs.at[s], gcr.at[s], sibling)
        last.append(copy)
    sent += last
    for copy in tap_back:
        copy.wait_recv()
    for block in range(4):
        tap_out[:, block * 128 : (block + 1) * 128] = tap_full[block * 32 : block * 32 + 32, :]
    for copy in last:
        copy.wait_recv()
    for g in range(4):
        for block in range(4):
            at = (g * 4 + block) * 512
            out_ref[g, :, block * 128 : (block + 1) * 128] = full[at : at + 512, :]
    for copy in sent:
        copy.wait_send()


def summed_over_devices(tap_term, query_term, key_term, value_term, out_term, scale):
    taps, width = tap_term.shape
    tap_rows = jnp.pad(tap_term, ((0, 32 - taps), (0, 0)))
    bf16, full32 = jnp.bfloat16, jnp.float32
    dma = pltpu.SemaphoreType.DMA
    grads, tap_sum = pl.pallas_call(
        functools.partial(sum_kernel, scale),
        out_shape=(
            jax.ShapeDtypeStruct((4, width, width), bf16),
            jax.ShapeDtypeStruct((32, width), full32),
        ),
        in_specs=[pl.BlockSpec(memory_space=pltpu.VMEM)] * 5,
        out_specs=[pl.BlockSpec(memory_space=pltpu.VMEM)] * 2,
        scratch_shapes=[
            pltpu.VMEM((2 * HALF, 128), bf16),
            pltpu.VMEM((2 * HALF, 128), bf16),
            pltpu.VMEM((2, STREAM, 128), bf16),
            pltpu.VMEM((2, 3, FIRST, 128), bf16),
            pltpu.VMEM((2, 3, SECOND, 128), bf16),
            pltpu.VMEM((2, NZ - 1, TILE, 128), bf16),
            pltpu.VMEM((128, 128), full32),
            pltpu.VMEM((NZ - 1, 16, 128), full32),
            pltpu.VMEM((10, 16, 128), full32),
            pltpu.VMEM((128, 128), full32),
            dma((2,)),
            dma((2,)),
            dma((2, 3)),
            dma((2, 3)),
            dma((2, 3)),
            dma((2, 3)),
            dma((2, NZ - 1)),
            dma((2, NZ - 1)),
            dma((2, NZ + 5)),
            dma((2, NZ + 5)),
            dma((2,)),
            dma((2,)),
            dma((NZ + 8,)),
            dma((NZ + 8,)),
            dma((NZ - 1,)),
            dma((NZ - 1,)),
        ],
        compiler_params=pltpu.CompilerParams(
            collective_id=0, has_side_effects=True, vmem_limit_bytes=40 * 2**20
        ),
    )(query_term, key_term, value_term, out_term, tap_rows)
    return (tap_sum[:taps],) + tuple(f32(grads[g]) for g in range(4))


def extended(array, sides, width):
    for axis, dim in sides:
        size, length = (lax.axis_size(axis), array.shape[dim])
        up = [(i, (i + 1) % size) for i in range(size - 1)]
        down = [(j, i) for i, j in up]
        last = lax.slice_in_dim(array, length - width, length, axis=dim)
        first = lax.slice_in_dim(array, 0, width, axis=dim)
        before = lax.ppermute(last, axis, up)
        after = lax.ppermute(first, axis, down)
        array = jnp.concatenate([before, array, after], axis=dim)
    return array


def depthwise(padded, kernel, length):
    summed = jnp.zeros((padded.shape[0], length, padded.shape[2]), jnp.float32)
    for offset in range(kernel.shape[0]):
        summed = (
            summed + padded[:, offset : offset + length, :].astype(jnp.float32) * kernel[offset]
        )
    return summed


def transposed(padded, kernel, length):
    reach = kernel.shape[0] - 1
    summed = jnp.zeros((padded.shape[0], length, padded.shape[2]), jnp.float32)
    for offset in range(kernel.shape[0]):
        start = reach - offset
        summed = summed + padded[:, start : start + length, :] * kernel[offset]
    return summed


def kernel_terms(padded, gradient, taps):
    length = gradient.shape[1]
    rows_out = []
    for offset in range(taps):
        rows_out.append(
            jnp.sum(
                padded[:, offset : offset + length, :].astype(jnp.float32) * gradient, axis=(0, 1)
            )
        )
    return jnp.stack(rows_out)


def split_heads(rows, head_count):
    first, length, width = rows.shape
    return rows.astype(jnp.float32).reshape(first, length, head_count, width // head_count)


def attend(queries, key_rows, value_rows, head_count):
    first, length, width = queries.shape
    factor = 1.0 / math.sqrt(width // head_count)
    query_heads = split_heads(queries, head_count)
    key_heads = split_heads(key_rows, head_count)
    value_heads = split_heads(value_rows, head_count)
    scores = jnp.einsum("athe,bthe->abth", query_heads, key_heads) * factor
    weights = jnp.exp(scores)
    weights = weights / jnp.sum(weights, axis=1, keepdims=True)
    mixed = jnp.einsum("abth,bthe->athe", weights, value_heads).reshape(first, length, width)
    return (mixed, weights)


def attend_back(queries, key_rows, value_rows, weights, upstream, head_count):
    first, length, width = queries.shape
    others = key_rows.shape[0]
    factor = 1.0 / math.sqrt(width // head_count)
    query_heads = split_heads(queries, head_count)
    key_heads = split_heads(key_rows, head_count)
    value_heads = split_heads(value_rows, head_count)
    up_heads = split_heads(upstream, head_count)
    products = jnp.einsum("athe,bthe->abth", up_heads, value_heads)
    inner = weights * (products - jnp.sum(weights * products, axis=1, keepdims=True)) * factor
    dquery = jnp.einsum("abth,bthe->athe", inner, key_heads).reshape(first, length, width)
    key_terms = jnp.einsum("abth,athe->bthe", inner, query_heads).reshape(others, length, width)
    value_terms = jnp.einsum("abth,athe->bthe", weights, up_heads).reshape(others, length, width)
    return (dquery, key_terms, value_terms)


def project(inputs, matrix):
    width = inputs.shape[-1]
    return jnp.dot(inputs.reshape(-1, width), matrix, preferred_element_type=jnp.float32).reshape(
        inputs.shape[:-1] + (matrix.shape[1],)
    )


def outer(left, right):
    width = left.shape[-1]
    return jnp.dot(
        left.reshape(-1, width).T,
        right.reshape(-1, right.shape[-1]),
        preferred_element_type=jnp.float32,
    )


def shards(frames, cotangent, kernel, w_query, w_key, w_value, w_out):
    reach = kernel.shape[0] // 2
    length = frames.shape[1]
    count = frames.shape[0]
    padded = extended(frames, (("tm", 1),), reach)
    conv = depthwise(padded, kernel, length)
    acted = jax.nn.silu(conv).astype(jnp.bfloat16)
    queries = project(acted, w_query).astype(jnp.bfloat16)
    key_rows = project(acted, w_key).astype(jnp.bfloat16)
    value_rows = project(acted, w_value).astype(jnp.bfloat16)
    key_all, value_all = (
        lax.all_gather(key_rows, "mic", axis=0, tiled=True),
        lax.all_gather(value_rows, "mic", axis=0, tiled=True),
    )
    mixed, weights = attend(queries, key_all, value_all, HEADS)
    mixed = mixed.astype(jnp.bfloat16)
    upstream = project(cotangent, w_out.T).astype(jnp.bfloat16)
    dquery, key_terms, value_terms = attend_back(
        queries, key_all, value_all, weights, upstream, HEADS
    )
    key_sum, value_sum = (
        lax.psum_scatter(key_terms, "mic", scatter_dimension=0, tiled=True),
        lax.psum_scatter(value_terms, "mic", scatter_dimension=0, tiled=True),
    )
    layer_out = (frames.astype(jnp.float32) + project(mixed, w_out)).astype(jnp.bfloat16)
    out_term = outer(mixed, cotangent)
    dquery = dquery.astype(jnp.bfloat16)
    dkey = key_sum.astype(jnp.bfloat16)
    dvalue = value_sum.astype(jnp.bfloat16)
    query_term = outer(acted, dquery)
    key_term = outer(acted, dkey)
    value_term = outer(acted, dvalue)
    dacted = project(dquery, w_query.T) + project(dkey, w_key.T) + project(dvalue, w_value.T)
    sig = jax.nn.sigmoid(conv)
    dconv = dacted * sig * (1.0 + conv * (1.0 - sig))
    grad_pad = extended(dconv.astype(jnp.bfloat16), (("tm", 1),), reach).astype(dconv.dtype)
    frame_grad = (cotangent.astype(jnp.float32) + transposed(grad_pad, kernel, length)).astype(
        jnp.bfloat16
    )
    tap_term = kernel_terms(padded, dconv, kernel.shape[0])
    norm_factor = 1.0 / math.sqrt(lax.axis_size("mic") * count * lax.axis_size("tm") * length)
    kernel_grad, query_grad, key_grad, value_grad, out_grad = summed_over_devices(
        tap_term, query_term, key_term, value_term, out_term, norm_factor
    )
    return (layer_out, frame_grad, kernel_grad, query_grad, key_grad, value_grad, out_grad)


def solution(mesh):
    in_specs = (P("mic", "tm", None), P("mic", "tm", None), P(), P(), P(), P(), P())
    out_specs = (P("mic", "tm", None), P("mic", "tm", None), P(), P(), P(), P(), P())
    return jax.shard_map(shards, mesh=mesh, in_specs=in_specs, out_specs=out_specs, check_vma=False)
```

```python
import math
import types

import jax
import jax.numpy as jnp
from jax import lax
from jax.experimental import pallas as pl
from jax.experimental.pallas import tpu as pltpu
from jax.sharding import PartitionSpec as P

HEADS = 8
FRAMES = 128
SHARE = 32
NX, NY, NZ = 4, 4, 8
MESH = pl.DeviceIdType.MESH


class Place:
    def __init__(self):
        mic = lax.axis_index("mic")
        tm = lax.axis_index("tm")
        self.mic, self.tm = mic, tm
        self.core = lax.rem(mic, 2)
        self.x = lax.rem(tm, NX)
        self.z = lax.rem(lax.div(tm, NX), NZ)
        self.y = lax.div(tm, NX * NZ) * 2 + lax.div(mic, 2)

    def device(self, x=None, y=None, z=None, core=None):
        x = self.x if x is None else x
        y = self.y if y is None else y
        z = self.z if z is None else z
        core = self.core if core is None else core
        mic = lax.rem(y, 2) * 2 + core
        tm = lax.div(y, 2) * (NX * NZ) + z * NX + x
        return (mic, tm)

    def along(self, axis, step):
        size = {"x": NX, "y": NY, "z": NZ, "core": 2}[axis]
        index = lax.rem(getattr(self, axis) + step, size)
        return index, self.device(**{axis: index})


def rows_at(start, count):
    return pl.ds(pl.multiple_of(start, count), count)


def send(src, dst, send_sem, recv_sem, device):
    copy = pltpu.make_async_remote_copy(
        src_ref=src,
        dst_ref=dst,
        send_sem=send_sem,
        recv_sem=recv_sem,
        device_id=device,
        device_id_type=MESH,
    )
    copy.start()
    return copy


def greet(peers):
    barrier = pltpu.get_barrier_semaphore()
    for peer in peers:
        pl.semaphore_signal(barrier, inc=1, device_id=peer, device_id_type=MESH)
    pl.semaphore_wait(barrier, len(peers))


SIZES = {"x": NX, "y": NY, "z": NZ, "core": 2}
HALF, STREAM, FIRST, SECOND, TILE = 4096, 2048, 512, 128, 16
ORDERS = (("x", "y", "z"), ("y", "x", "z"))


def f32(value):
    return value.astype(jnp.float32)


def dot(left, right, left_dim=1, right_dim=0):
    return lax.dot_general(
        left, right, (((left_dim,), (right_dim,)), ((), ())), preferred_element_type=jnp.float32
    )


def lanes(block):
    return pl.ds(pl.multiple_of(block * 128, 128), 128)


def shifted(padded):
    for low in range(8):
        rolled = padded if low == 0 else pltpu.roll(padded, padded.shape[0] - low, 0)
        for high in range(4):
            if high * 8 + low:
                yield high * 8 + low, rolled[high * 8 : high * 8 + FRAMES, :]


def kernel_body(
    scale,
    frames,
    cotangent,
    taps,
    w_query,
    w_key,
    w_value,
    w_out,
    layer_out,
    frame_grad,
    tap_out,
    grads_out,
    m,
):
    bf16 = jnp.bfloat16
    here = Place()
    group = [lax.rem(here.mic + step, 4) for step in range(1, 4)]
    after = (here.mic, lax.rem(here.tm + 1, NX * NY * NZ // 2))
    before = (here.mic, lax.rem(here.tm + NX * NY * NZ // 2 - 1, NX * NY * NZ // 2))
    peers = [after, before]
    peers += [(mic, here.tm) for mic in group]
    for axis in ("core", "x", "y", "z"):
        for step in range(1, SIZES[axis]):
            peers.append(here.along(axis, step)[1])
    greet(peers)
    sent = []

    halo = [
        send(frames.at[:, pl.ds(FRAMES - 16, 16), :], m.halo.at[0], m.hs.at[0], m.hr.at[0], after),
        send(frames.at[:, pl.ds(0, 16), :], m.halo.at[1], m.hs.at[1], m.hr.at[1], before),
    ]
    mics_here = pl.ds(here.mic * 2, 2)
    share_here = rows_at(here.mic * SHARE, SHARE)
    cot_copies = []
    for step, mic in enumerate(group):
        cot_copies.append(
            send(
                cotangent.at[:, rows_at(mic * SHARE, SHARE), :],
                m.cot_all.at[mics_here],
                m.cs.at[step],
                m.cr.at[step],
                (mic, here.tm),
            )
        )
    sent += halo + cot_copies
    m.cot_all[mics_here] = cotangent[:, share_here, :]
    for block in range(4):
        m.taps4[block, 0:31] = taps[:, block * 128 : (block + 1) * 128]
        for mic in range(2):
            m.fpad[mic, block, 16 : 16 + FRAMES] = f32(
                frames[mic, :, block * 128 : (block + 1) * 128]
            )
    row = lax.broadcasted_iota(jnp.int32, (512, 128), 0)
    col = lax.broadcasted_iota(jnp.int32, (512, 128), 1)
    m.gather_heads[...] = jnp.where(lax.div(row, 64) == col, 1.0, 0.0).astype(bf16)
    row = lax.broadcasted_iota(jnp.int32, (128, 512), 0)
    col = lax.broadcasted_iota(jnp.int32, (128, 512), 1)
    m.spread_heads[...] = jnp.where(lax.div(col, 64) == row, 1.0, 0.0).astype(bf16)

    def fill_halo(side, pad, buffer, copy):
        copy.wait_recv()
        inside = here.tm > 0 if side == 0 else here.tm < NX * NY * NZ // 2 - 1
        rows = slice(0, 16) if side == 0 else slice(16 + FRAMES, 32 + FRAMES)
        for mic in range(2):
            for block in range(4):
                value = f32(buffer[side, mic, :, block * 128 : (block + 1) * 128])
                pad[mic, block, rows] = jnp.where(inside, value, 0.0)

    for side in range(2):
        fill_halo(side, m.fpad, m.halo, halo[side])

    act_copies = []
    for mic in range(2):

        def conv_block(block, carry):
            padded = m.fpad[mic, block]
            conv = jnp.zeros((FRAMES, 128), jnp.float32)
            for offset, rows in shifted(padded):
                conv = conv + rows * m.taps4[block, offset - 1 : offset]
            sig = 1.0 / (1.0 + jnp.exp(-conv))
            m.acted[mic, :, lanes(block)] = (conv * sig).astype(bf16)
            m.dsilu[mic, block] = sig * (1.0 + conv * (1.0 - sig))
            return carry

        lax.fori_loop(0, 4, conv_block, 0)
        for step, target in enumerate(group):
            act_copies.append(
                send(
                    m.acted.at[mic, rows_at(target * SHARE, SHARE), :],
                    m.act_all.at[here.mic * 2 + mic],
                    m.acs.at[mic, step],
                    m.acr.at[mic, step],
                    (target, here.tm),
                )
            )
        m.act_all[here.mic * 2 + mic] = m.acted[mic, share_here, :]
    sent += act_copies

    width = frames.shape[2]
    rows = 8 * SHARE
    for copy in cot_copies:
        copy.wait_recv()
    cot_rows = m.cot_all[...].reshape(rows, width)
    m.ups[...] = dot(cot_rows, w_out[...], 1, 1).astype(bf16).reshape(8, SHARE, width)
    for copy in act_copies:
        copy.wait_recv()
    act_rows = m.act_all[...].reshape(rows, width)
    for weight, target in ((w_query, m.queries), (w_key, m.keys), (w_value, m.values)):
        target[...] = dot(act_rows, weight[...]).astype(bf16).reshape(8, SHARE, width)

    m.dkey[...] = jnp.zeros_like(m.dkey)
    m.dvalue[...] = jnp.zeros_like(m.dvalue)
    factor = 1.0 / math.sqrt(width // HEADS)

    def attend(index, carry):
        query, up = m.queries[index], m.ups[index]
        keys, values = m.keys[...], m.values[...]
        gather, spread = m.gather_heads[...], m.spread_heads[...]

        def per_head(product):
            return dot(product.reshape(rows, width), gather).reshape(8, SHARE, 128)

        def per_lane(heads):
            return dot(heads.astype(bf16).reshape(rows, 128), spread).reshape(8, SHARE, width)

        weights = jnp.exp(per_head(query[None] * keys) * factor)
        weights = weights / jnp.sum(weights, axis=0, keepdims=True)
        products = per_head(up[None] * values)
        inner = weights * (products - jnp.sum(weights * products, axis=0, keepdims=True)) * factor
        weights, inner = per_lane(weights), per_lane(inner)
        m.mixed[index] = jnp.sum(weights * f32(values), axis=0).astype(bf16)
        m.dquery[index] = jnp.sum(inner * f32(keys), axis=0).astype(bf16)
        m.dkey[...] += inner * f32(query)[None]
        m.dvalue[...] += weights * f32(up)[None]
        return carry

    lax.fori_loop(0, 8, attend, 0)

    mixed = m.mixed[...].reshape(rows, width)
    dquery = m.dquery[...].reshape(rows, width)
    dkey = m.dkey[...].astype(bf16).reshape(rows, width)
    dvalue = m.dvalue[...].astype(bf16).reshape(rows, width)
    dacted = dot(dquery, w_query[...], 1, 1)
    dacted = dacted + dot(dkey, w_key[...], 1, 1)
    dacted = dacted + dot(dvalue, w_value[...], 1, 1)
    m.dacted[...] = dacted.astype(bf16).reshape(8, SHARE, width)
    home_copies = []
    for kind, (source, target) in enumerate(((m.dacted, m.dacted_home), (m.mixed, m.mixed_home))):
        copies = []
        for step, mic in enumerate(group):
            copies.append(
                send(
                    source.at[pl.ds(mic * 2, 2)],
                    target.at[:, share_here, :],
                    m.bs.at[kind, step],
                    m.br.at[kind, step],
                    (mic, here.tm),
                )
            )
        target[:, share_here, :] = source[mics_here]
        home_copies.append(copies)
        sent += copies

    act_turned = act_rows.T
    for g, (left, right) in enumerate(
        ((act_turned, dquery), (act_turned, dkey), (act_turned, dvalue), (mixed.T, cot_rows))
    ):
        term = dot(left, right).astype(bf16)
        for block in range(4):
            at = (g * 4 + block) * 512
            m.mine[at : at + 512, :] = term[:, block * 128 : (block + 1) * 128]

    own = here.core * HALF
    other, sibling = here.along("core", 1)
    core_copies = []
    for s in range(2):
        core_copies.append(
            send(
                m.mine.at[rows_at(other * HALF + s * STREAM, STREAM)],
                m.core_rx.at[s],
                m.core_s.at[s],
                m.core_r.at[s],
                sibling,
            )
        )
    sent += core_copies

    for copy in home_copies[0]:
        copy.wait_recv()

    def dconv_block(step, carry):
        mic, block = lax.div(step, 4), lax.rem(step, 4)
        dconv = f32(m.dacted_home[mic, :, lanes(block)]) * m.dsilu[mic, block]
        m.gpad[mic, block, 16 : 16 + FRAMES] = dconv
        m.ends[0, mic, :, lanes(block)] = dconv[FRAMES - 16 :].astype(bf16)
        m.ends[1, mic, :, lanes(block)] = dconv[:16].astype(bf16)
        return carry

    lax.fori_loop(0, 8, dconv_block, 0)
    ghalo = [
        send(m.ends.at[0], m.ghalo.at[0], m.hs.at[2], m.hr.at[2], after),
        send(m.ends.at[1], m.ghalo.at[1], m.hs.at[3], m.hr.at[3], before),
    ]
    sent += ghalo

    first = []
    for s in range(2):
        core_copies[s].wait_recv()
        part = rows_at(own + s * STREAM, STREAM)
        m.mine[part, :] = (f32(m.mine[part, :]) + f32(m.core_rx[s])).astype(bf16)
        axis = ORDERS[s][0]
        copies = []
        for step in range(1, SIZES[axis]):
            index, peer = here.along(axis, step)
            copies.append(
                send(
                    m.mine.at[rows_at(own + s * STREAM + index * FIRST, FIRST)],
                    m.rx1.at[s, step - 1],
                    m.s1.at[s, step - 1],
                    m.r1.at[s, step - 1],
                    peer,
                )
            )
        first.append(copies)
        sent += copies

    def tap_block(block, carry):
        sums = {}
        for mic in range(2):
            dconv = m.gpad[mic, block, 16 : 16 + FRAMES]
            for offset, rows_in in shifted(m.fpad[mic, block]):
                part = jnp.sum((rows_in * dconv).reshape(FRAMES // 8, 8, 128), axis=0)
                sums[offset] = sums[offset] + part if mic else part
        for offset, part in sums.items():
            m.tap0[block, offset - 1 : offset] = jnp.sum(part, axis=0, keepdims=True)
        m.tap0[block, 31:32] = jnp.zeros((1, 128), jnp.float32)
        return carry

    lax.fori_loop(0, 4, tap_block, 0)

    def tap_tile(index):
        return lax.div(index, 2), rows_at(lax.rem(index, 2) * 16, 16)

    tap_copies = []
    for step in range(1, NZ):
        index, peer = here.along("z", step)
        block, part = tap_tile(index)
        tap_copies.append(
            send(
                m.tap0.at[block, part],
                m.tap_zrx.at[step - 1],
                m.ts.at[step - 1],
                m.tr.at[step - 1],
                peer,
            )
        )
    sent += tap_copies

    for copy in home_copies[1]:
        copy.wait_recv()
    home_rows = m.mixed_home[...].reshape(2 * FRAMES, width)
    layer_out[...] = (
        f32(frames[...]) + dot(home_rows, w_out[...]).reshape(2, FRAMES, width)
    ).astype(bf16)

    second = []
    for s in range(2):
        axis, axis2, _ = ORDERS[s]
        place = own + s * STREAM + getattr(here, axis) * FIRST
        for copy in first[s]:
            copy.wait_recv()
        part = rows_at(place, FIRST)
        total = f32(m.mine[part, :])
        for step in range(SIZES[axis] - 1):
            total = total + f32(m.rx1[s, step])
        m.mine[part, :] = total.astype(bf16)
        copies = []
        for step in range(1, SIZES[axis2]):
            index, peer = here.along(axis2, step)
            copies.append(
                send(
                    m.mine.at[rows_at(place + index * SECOND, SECOND)],
                    m.rx2.at[s, step - 1],
                    m.s2.at[s, step - 1],
                    m.r2.at[s, step - 1],
                    peer,
                )
            )
        second.append((place, copies))
        sent += copies

    block, part = tap_tile(here.z)
    total = m.tap0[block, part]
    for step in range(1, NZ):
        tap_copies[step - 1].wait_recv()
        total = total + m.tap_zrx[step - 1]

    def tap_axis(tile, axis, base):
        slot = base + getattr(here, axis)
        m.tap_rx[slot] = tile
        copies = []
        for step in range(1, SIZES[axis]):
            copies.append(
                send(
                    m.tap_rx.at[slot],
                    m.tap_rx.at[slot],
                    m.ts.at[NZ - 1 + base + step - 1],
                    m.tr.at[NZ - 1 + base + step - 1],
                    here.along(axis, step)[1],
                )
            )
        return copies

    def tap_sum(copies, base):
        for copy in copies:
            copy.wait_recv()
        total = m.tap_rx[base]
        for index in range(len(copies)):
            total = total + m.tap_rx[base + 1 + index]
        return total

    tap_x = tap_axis(total, "x", 0)
    sent += tap_x

    for side in range(2):
        fill_halo(side, m.gpad, m.ghalo, ghalo[side])

    def grad_block(step, carry):
        mic, block = lax.div(step, 4), lax.rem(step, 4)
        total = f32(cotangent[mic, :, lanes(block)])
        for offset, rows_in in shifted(m.gpad[mic, block]):
            total = total + rows_in * m.taps4[block, 31 - offset : 32 - offset]
        frame_grad[mic, :, lanes(block)] = total.astype(bf16)
        return carry

    lax.fori_loop(0, 8, grad_block, 0)

    third = []
    for s in range(2):
        axis2 = ORDERS[s][1]
        place, copies = second[s]
        place = place + getattr(here, axis2) * SECOND
        for copy in copies:
            copy.wait_recv()
        part = rows_at(place, SECOND)
        total = f32(m.mine[part, :])
        for step in range(SIZES[axis2] - 1):
            total = total + f32(m.rx2[s, step])
        m.mine[part, :] = total.astype(bf16)
        copies = []
        for step in range(1, NZ):
            index, peer = here.along("z", step)
            copies.append(
                send(
                    m.mine.at[rows_at(place + index * TILE, TILE)],
                    m.rx3.at[s, step - 1],
                    m.s3.at[s, step - 1],
                    m.r3.at[s, step - 1],
                    peer,
                )
            )
        third.append((place, copies))
        sent += copies

    tap_y = tap_axis(tap_sum(tap_x, 0), "y", 4)
    sent += tap_y

    def gather(s, level, axis, place, count):
        copies = []
        base = (0, NZ - 1, NZ + 2)[level]
        part = rows_at(place, count)
        for step in range(1, SIZES[axis]):
            copies.append(
                send(
                    m.full.at[part],
                    m.full.at[part],
                    m.gs.at[s, base + step - 1],
                    m.gr.at[s, base + step - 1],
                    here.along(axis, step)[1],
                )
            )
        return copies

    back = []
    for s in range(2):
        place, copies = third[s]
        for copy in copies:
            copy.wait_recv()
        part = rows_at(place + here.z * TILE, TILE)
        total = f32(m.mine[part, :])
        for step in range(NZ - 1):
            total = total + f32(m.rx3[s, step])
        m.full[part, :] = (total * scale).astype(bf16)
        copies = gather(s, 0, "z", place + here.z * TILE, TILE)
        back.append((place, copies))
        sent += copies

    tap_c = tap_axis(tap_sum(tap_y, 4), "core", 8)
    sent += tap_c

    for level in (1, 2):
        for s in range(2):
            place, copies = back[s]
            for copy in copies:
                copy.wait_recv()
            axis = ORDERS[s][2 - level]
            count = (TILE, SECOND, FIRST)[level]
            copies = gather(s, level, axis, place, count)
            back[s] = (place - getattr(here, axis) * count, copies)
            sent += copies
        if level == 1:
            block, part = tap_tile(here.z)
            m.tap_full[block, part] = tap_sum(tap_c, 8) * scale
            tap_back = []
            for step in range(1, NZ):
                tap_back.append(
                    send(
                        m.tap_full.at[block, part],
                        m.tap_full.at[block, part],
                        m.tgs.at[step - 1],
                        m.tgr.at[step - 1],
                        here.along("z", step)[1],
                    )
                )
            sent += tap_back
    last = []
    for s in range(2):
        place, copies = back[s]
        for copy in copies:
            copy.wait_recv()
        part = rows_at(own + s * STREAM, STREAM)
        copy = send(m.full.at[part], m.full.at[part], m.gcs.at[s], m.gcr.at[s], sibling)
        last.append(copy)
    sent += last
    for copy in tap_back:
        copy.wait_recv()
    for block in range(4):
        tap_out[:, block * 128 : (block + 1) * 128] = m.tap_full[block, 0:31]
    for copy in last:
        copy.wait_recv()
    for g in range(4):
        for block in range(4):
            at = (g * 4 + block) * 512
            grads_out[g, :, block * 128 : (block + 1) * 128] = m.full[at : at + 512, :]
    for copy in sent:
        copy.wait_send()


def memory(width):
    bf16, full = jnp.bfloat16, jnp.float32
    dma = pltpu.SemaphoreType.DMA
    rows = (8, SHARE, width)
    home = (2, FRAMES, width)
    wide = (2, 4, FRAMES + 32, 128)
    return dict(
        halo=pltpu.VMEM((2, 2, 16, width), bf16),
        ghalo=pltpu.VMEM((2, 2, 16, width), bf16),
        ends=pltpu.VMEM((2, 2, 16, width), bf16),
        cot_all=pltpu.VMEM(rows, bf16),
        act_all=pltpu.VMEM(rows, bf16),
        acted=pltpu.VMEM(home, bf16),
        taps4=pltpu.VMEM((4, 32, 128), full),
        fpad=pltpu.VMEM(wide, full),
        gpad=pltpu.VMEM(wide, full),
        dsilu=pltpu.VMEM((2, 4, FRAMES, 128), full),
        gather_heads=pltpu.VMEM((width, 128), bf16),
        spread_heads=pltpu.VMEM((128, width), bf16),
        queries=pltpu.VMEM(rows, bf16),
        keys=pltpu.VMEM(rows, bf16),
        values=pltpu.VMEM(rows, bf16),
        ups=pltpu.VMEM(rows, bf16),
        mixed=pltpu.VMEM(rows, bf16),
        dquery=pltpu.VMEM(rows, bf16),
        dkey=pltpu.VMEM(rows, full),
        dvalue=pltpu.VMEM(rows, full),
        dacted=pltpu.VMEM(rows, bf16),
        dacted_home=pltpu.VMEM(home, bf16),
        mixed_home=pltpu.VMEM(home, bf16),
        mine=pltpu.VMEM((2 * HALF, 128), bf16),
        full=pltpu.VMEM((2 * HALF, 128), bf16),
        core_rx=pltpu.VMEM((2, STREAM, 128), bf16),
        rx1=pltpu.VMEM((2, 3, FIRST, 128), bf16),
        rx2=pltpu.VMEM((2, 3, SECOND, 128), bf16),
        rx3=pltpu.VMEM((2, NZ - 1, TILE, 128), bf16),
        tap0=pltpu.VMEM((4, 32, 128), full),
        tap_zrx=pltpu.VMEM((NZ - 1, 16, 128), full),
        tap_rx=pltpu.VMEM((10, 16, 128), full),
        tap_full=pltpu.VMEM((4, 32, 128), full),
        hs=dma((4,)),
        hr=dma((4,)),
        cs=dma((3,)),
        cr=dma((3,)),
        acs=dma((2, 3)),
        acr=dma((2, 3)),
        bs=dma((2, 3)),
        br=dma((2, 3)),
        core_s=dma((2,)),
        core_r=dma((2,)),
        s1=dma((2, 3)),
        r1=dma((2, 3)),
        s2=dma((2, 3)),
        r2=dma((2, 3)),
        s3=dma((2, NZ - 1)),
        r3=dma((2, NZ - 1)),
        gs=dma((2, NZ + 5)),
        gr=dma((2, NZ + 5)),
        gcs=dma((2,)),
        gcr=dma((2,)),
        ts=dma((NZ + 8,)),
        tr=dma((NZ + 8,)),
        tgs=dma((NZ - 1,)),
        tgr=dma((NZ - 1,)),
    )


def shards(frames, cotangent, kernel, w_query, w_key, w_value, w_out):
    count, length, width = frames.shape
    scale = 1.0 / math.sqrt(lax.axis_size("mic") * count * lax.axis_size("tm") * length)
    scratch = memory(width)

    def body(*refs):
        parts = types.SimpleNamespace(**dict(zip(scratch, refs[11:])))
        kernel_body(scale, *refs[:11], parts)

    layer_out, frame_grad, kernel_grad, grads = pl.pallas_call(
        body,
        out_shape=(
            jax.ShapeDtypeStruct(frames.shape, jnp.bfloat16),
            jax.ShapeDtypeStruct(frames.shape, jnp.bfloat16),
            jax.ShapeDtypeStruct(kernel.shape, jnp.float32),
            jax.ShapeDtypeStruct((4, width, width), jnp.bfloat16),
        ),
        in_specs=[pl.BlockSpec(memory_space=pltpu.VMEM)] * 7,
        out_specs=[pl.BlockSpec(memory_space=pltpu.VMEM)] * 4,
        scratch_shapes=list(scratch.values()),
        compiler_params=pltpu.CompilerParams(
            collective_id=0, has_side_effects=True, vmem_limit_bytes=56 * 2**20
        ),
    )(frames, cotangent, kernel, w_query, w_key, w_value, w_out)
    return (layer_out, frame_grad, kernel_grad) + tuple(f32(grads[g]) for g in range(4))


def solution(mesh):
    in_specs = (P("mic", "tm", None), P("mic", "tm", None), P(), P(), P(), P(), P())
    out_specs = (P("mic", "tm", None), P("mic", "tm", None), P(), P(), P(), P(), P())
    return jax.shard_map(shards, mesh=mesh, in_specs=in_specs, out_specs=out_specs, check_vma=False)
```

```python
import math
import types

import jax
import jax.numpy as jnp
from jax import lax
from jax.experimental import pallas as pl
from jax.experimental.pallas import tpu as pltpu
from jax.sharding import PartitionSpec as P

HEADS = 8
FRAMES = 128
SHARE = 32
NX, NY, NZ = 4, 4, 8
MESH = pl.DeviceIdType.MESH


class Place:
    def __init__(self):
        mic = lax.axis_index("mic")
        tm = lax.axis_index("tm")
        self.mic, self.tm = mic, tm
        self.core = lax.rem(mic, 2)
        self.x = lax.rem(tm, NX)
        self.z = lax.rem(lax.div(tm, NX), NZ)
        self.y = lax.div(tm, NX * NZ) * 2 + lax.div(mic, 2)

    def device(self, x=None, y=None, z=None, core=None):
        x = self.x if x is None else x
        y = self.y if y is None else y
        z = self.z if z is None else z
        core = self.core if core is None else core
        mic = lax.rem(y, 2) * 2 + core
        tm = lax.div(y, 2) * (NX * NZ) + z * NX + x
        return (mic, tm)

    def along(self, axis, step):
        size = {"x": NX, "y": NY, "z": NZ, "core": 2}[axis]
        index = lax.rem(getattr(self, axis) + step, size)
        return index, self.device(**{axis: index})


def rows_at(start, count):
    return pl.ds(pl.multiple_of(start, count), count)


def send(src, dst, send_sem, recv_sem, device):
    copy = pltpu.make_async_remote_copy(
        src_ref=src,
        dst_ref=dst,
        send_sem=send_sem,
        recv_sem=recv_sem,
        device_id=device,
        device_id_type=MESH,
    )
    copy.start()
    return copy


def local(src, dst, sem):
    copy = pltpu.make_async_copy(src, dst, sem)
    copy.start()
    return copy


SIZES = {"x": NX, "y": NY, "z": NZ, "core": 2}
HALF, STREAM, FIRST, SECOND, TILE = 4096, 2048, 512, 128, 16
ORDERS = (("x", "y", "z"), ("y", "x", "z"))


ACT, ACT_S, MIXED, DQUERY, DKEY, DVALUE, COT, COT_S, FIRST_S, SECOND_S = range(10)


def f32(value):
    return value.astype(jnp.float32)


def dot(left, right, left_dim=1, right_dim=0):
    return lax.dot_general(
        left, right, (((left_dim,), (right_dim,)), ((), ())), preferred_element_type=jnp.float32
    )


def lanes(block):
    return pl.ds(pl.multiple_of(block * 128, 128), 128)


def shifted(padded, mic, block, base, count):
    for offset in range(1, 32):
        yield offset, padded[mic, block, base + offset : base + offset + count]


def kernel_body(
    scale,
    frames,
    cotangent,
    taps,
    w_query,
    w_key,
    w_value,
    w_out,
    layer_out,
    frame_grad,
    tap_out,
    grads_out,
    m,
):
    bf16 = jnp.bfloat16
    here = Place()
    width = frames.shape[2]
    rows = 8 * SHARE
    count = NX * NY * NZ // 2
    group = [lax.rem(here.mic + step, 4) for step in range(1, 4)]
    after = (here.mic, lax.rem(here.tm + 1, count))
    before = (here.mic, lax.rem(here.tm + count - 1, count))
    peers = [after, before]
    peers += [(mic, here.tm) for mic in group]
    for axis in ("core", "x", "y", "z"):
        for step in range(1, SIZES[axis]):
            peers.append(here.along(axis, step)[1])
    barrier = pltpu.get_barrier_semaphore()
    for peer in peers:
        pl.semaphore_signal(barrier, inc=1, device_id=peer, device_id_type=MESH)
    loads = {}
    for at, (name, source) in enumerate(
        (
            ("frames", frames),
            ("taps", taps),
            ("cot", cotangent),
            ("w_out", w_out),
            ("w_query", w_query),
            ("w_key", w_key),
            ("w_value", w_value),
        )
    ):
        loads[name] = local(source, getattr(m, name), m.load.at[at])
    pl.semaphore_wait(barrier, len(peers))
    sent = []

    halo = [
        send(frames.at[:, pl.ds(FRAMES - 16, 16), :], m.halo.at[0], m.hs.at[0], m.hr.at[0], after),
        send(frames.at[:, pl.ds(0, 16), :], m.halo.at[1], m.hs.at[1], m.hr.at[1], before),
    ]
    mics_here = pl.ds(here.mic * 2, 2)
    share_here = rows_at(here.mic * SHARE, SHARE)
    cot_copies = []
    for step, mic in enumerate(group):
        cot_copies.append(
            send(
                cotangent.at[:, rows_at(mic * SHARE, SHARE), :],
                m.pool.at[COT, mics_here],
                m.cs.at[step],
                m.cr.at[step],
                (mic, here.tm),
            )
        )
    sent += halo + cot_copies
    loads["frames"].wait()
    loads["taps"].wait()
    for block in range(4):
        m.taps4[block, 0:31] = m.taps[:, block * 128 : (block + 1) * 128]
        for mic in range(2):
            m.fpad[mic, block, 16 : 16 + FRAMES] = f32(
                m.frames[mic, :, block * 128 : (block + 1) * 128]
            )

    def conv_rows(mic, block, base, number):
        conv = jnp.zeros((number, 128), jnp.float32)
        for offset, part in shifted(m.fpad, mic, block, base, number):
            conv = conv + part * m.taps4[block, offset - 1 : offset]
        sig = 1.0 / (1.0 + jnp.exp(-conv))
        m.acted[mic, base : base + number, lanes(block)] = (conv * sig).astype(bf16)
        m.dsilu[mic, block, base : base + number] = sig * (1.0 + conv * (1.0 - sig))

    def inner_block(step, carry):
        conv_rows(lax.div(step, 4), lax.rem(step, 4), 16, FRAMES - 32)
        return carry

    lax.fori_loop(0, 8, inner_block, 0)

    row = lax.broadcasted_iota(jnp.int32, (512, 128), 0)
    col = lax.broadcasted_iota(jnp.int32, (512, 128), 1)
    m.gather_heads[...] = jnp.where(lax.div(row, 64) == col, 1.0, 0.0).astype(bf16)
    row = lax.broadcasted_iota(jnp.int32, (128, 512), 0)
    col = lax.broadcasted_iota(jnp.int32, (128, 512), 1)
    m.spread_heads[...] = jnp.where(lax.div(col, 64) == row, 1.0, 0.0).astype(bf16)
    loads["cot"].wait()
    m.pool[COT, mics_here] = m.cot[:, share_here, :]

    def fill_halo(side, pad, buffer, copy):
        copy.wait_recv()
        inside = here.tm > 0 if side == 0 else here.tm < count - 1
        place = slice(0, 16) if side == 0 else slice(16 + FRAMES, 32 + FRAMES)
        for mic in range(2):
            for block in range(4):
                value = f32(buffer[side, mic, :, block * 128 : (block + 1) * 128])
                pad[mic, block, place] = jnp.where(inside, value, 0.0)

    for side in range(2):
        fill_halo(side, m.fpad, m.halo, halo[side])

    act_copies = []
    for mic in range(2):

        def outer_block(block, carry):
            conv_rows(mic, block, 0, 16)
            conv_rows(mic, block, FRAMES - 16, 16)
            return carry

        lax.fori_loop(0, 4, outer_block, 0)
        for step, target in enumerate(group):
            act_copies.append(
                send(
                    m.acted.at[mic, rows_at(target * SHARE, SHARE), :],
                    m.pool.at[ACT, here.mic * 2 + mic],
                    m.acs.at[mic, step],
                    m.acr.at[mic, step],
                    (target, here.tm),
                )
            )
        m.pool[ACT, here.mic * 2 + mic] = m.acted[mic, share_here, :]
    sent += act_copies

    other, sibling = here.along("core", 1)

    def to_sibling(source, target):
        copy = send(
            m.pool.at[source],
            m.pool.at[target],
            m.core_s.at[target],
            m.core_r.at[target],
            sibling,
        )
        sent.append(copy)
        return copy

    for copy in cot_copies:
        copy.wait_recv()
    shared = {COT_S: to_sibling(COT, COT_S)}
    cot_rows = m.pool[COT].reshape(rows, width)
    loads["w_out"].wait()
    m.ups[...] = dot(cot_rows, m.w_out[...], 1, 1).astype(bf16).reshape(8, SHARE, width)
    for name in ("w_query", "w_key", "w_value"):
        loads[name].wait()
    for copy in act_copies:
        copy.wait_recv()
    shared[ACT_S] = to_sibling(ACT, ACT_S)
    act_rows = m.pool[ACT].reshape(rows, width)
    for weight, target in ((m.w_query, m.queries), (m.w_key, m.keys), (m.w_value, m.values)):
        target[...] = dot(act_rows, weight[...]).astype(bf16).reshape(8, SHARE, width)

    m.dkey[...] = jnp.zeros_like(m.dkey)
    m.dvalue[...] = jnp.zeros_like(m.dvalue)
    factor = 1.0 / math.sqrt(width // HEADS)

    def attend(index, carry):
        query, up = m.queries[index], m.ups[index]
        keys, values = m.keys[...], m.values[...]
        gather, spread = m.gather_heads[...], m.spread_heads[...]

        def per_head(product):
            return dot(product.reshape(rows, width), gather).reshape(8, SHARE, 128)

        def per_lane(heads):
            return dot(heads.astype(bf16).reshape(rows, 128), spread).reshape(8, SHARE, width)

        weights = jnp.exp(per_head(query[None] * keys) * factor)
        weights = weights / jnp.sum(weights, axis=0, keepdims=True)
        products = per_head(up[None] * values)
        inner = weights * (products - jnp.sum(weights * products, axis=0, keepdims=True)) * factor
        weights, inner = per_lane(weights), per_lane(inner)
        m.pool[MIXED, index] = jnp.sum(weights * f32(values), axis=0).astype(bf16)
        m.pool[DQUERY, index] = jnp.sum(inner * f32(keys), axis=0).astype(bf16)
        m.dkey[...] += inner * f32(query)[None]
        m.dvalue[...] += weights * f32(up)[None]
        return carry

    lax.fori_loop(0, 8, attend, 0)

    shared[FIRST_S] = to_sibling(DQUERY - other, FIRST_S)
    m.pool[DKEY] = m.dkey[...].astype(bf16)
    m.pool[DVALUE] = m.dvalue[...].astype(bf16)
    shared[SECOND_S] = to_sibling(DKEY + other, SECOND_S)

    def pooled(index):
        return m.pool[index].reshape(rows, width)

    dacted = dot(pooled(DQUERY), m.w_query[...], 1, 1)
    dacted = dacted + dot(pooled(DKEY), m.w_key[...], 1, 1)
    dacted = dacted + dot(pooled(DVALUE), m.w_value[...], 1, 1)
    m.dacted[...] = dacted.astype(bf16).reshape(8, SHARE, width)
    def send_home(kind, source, target):
        copies = []
        for step, mic in enumerate(group):
            copies.append(
                send(
                    source.at[pl.ds(mic * 2, 2)],
                    target.at[:, share_here, :],
                    m.bs.at[kind, step],
                    m.br.at[kind, step],
                    (mic, here.tm),
                )
            )
        target[:, share_here, :] = source[mics_here]
        sent.extend(copies)
        return copies

    dacted_copies = send_home(0, m.dacted, m.dacted_home)

    core = here.core
    operands = (
        ((ACT, DQUERY + 2 * core), (ACT_S, FIRST_S + core)),
        ((2 * core, DKEY + 2 * core), (ACT_S + 7 * core, SECOND_S - 2 * core)),
    )
    terms = []
    for mine, _ in operands:
        terms.append(dot(pooled(mine[0]), pooled(mine[1]), 0, 0))
    for copy in shared.values():
        copy.wait_recv()
    first = []
    for s in range(2):
        _, theirs = operands[s]
        term = (terms[s] + dot(pooled(theirs[0]), pooled(theirs[1]), 0, 0)).astype(bf16)
        for block in range(4):
            at = s * STREAM + block * 512
            m.mine[at : at + 512, :] = term[:, block * 128 : (block + 1) * 128]
        axis = ORDERS[s][0]
        copies = []
        for step in (2, 1, 3):
            index, peer = here.along(axis, step)
            copies.append(
                send(
                    m.mine.at[rows_at(s * STREAM + index * FIRST, FIRST)],
                    m.rx1.at[s, step - 1],
                    m.s1.at[s, step - 1],
                    m.r1.at[s, step - 1],
                    peer,
                )
            )
        first.append(copies)
        sent += copies

    mixed_copies = send_home(1, m.pool.at[MIXED], m.mixed_home)

    for copy in dacted_copies:
        copy.wait_recv()

    def dconv_block(step, carry):
        mic, block = lax.div(step, 4), lax.rem(step, 4)
        dconv = f32(m.dacted_home[mic, :, lanes(block)]) * m.dsilu[mic, block]
        m.gpad[mic, block, 16 : 16 + FRAMES] = dconv
        m.ends[0, mic, :, lanes(block)] = dconv[FRAMES - 16 :].astype(bf16)
        m.ends[1, mic, :, lanes(block)] = dconv[:16].astype(bf16)
        return carry

    lax.fori_loop(0, 8, dconv_block, 0)
    ghalo = [
        send(m.ends.at[0], m.ghalo.at[0], m.hs.at[2], m.hr.at[2], after),
        send(m.ends.at[1], m.ghalo.at[1], m.hs.at[3], m.hr.at[3], before),
    ]
    sent += ghalo

    def tap_block(block, carry):
        sums = {}
        for mic in range(2):
            dconv = m.gpad[mic, block, 16 : 16 + FRAMES]
            for offset, part in shifted(m.fpad, mic, block, 0, FRAMES):
                part = jnp.sum((part * dconv).reshape(FRAMES // 8, 8, 128), axis=0)
                sums[offset] = sums[offset] + part if mic else part
        for offset, part in sums.items():
            m.tap0[block, offset - 1 : offset] = jnp.sum(part, axis=0, keepdims=True)
        m.tap0[block, 31:32] = jnp.zeros((1, 128), jnp.float32)
        return carry

    lax.fori_loop(0, 4, tap_block, 0)

    def tap_tile(index):
        return lax.div(index, 2), rows_at(lax.rem(index, 2) * 16, 16)

    tap_copies = []
    for step in range(1, NZ):
        index, peer = here.along("z", step)
        block, part = tap_tile(index)
        tap_copies.append(
            send(
                m.tap0.at[block, part],
                m.tap_zrx.at[step - 1],
                m.ts.at[step - 1],
                m.tr.at[step - 1],
                peer,
            )
        )
    sent += tap_copies

    for side in range(2):
        fill_halo(side, m.gpad, m.ghalo, ghalo[side])

    def grad_block(step, carry):
        mic, block = lax.div(step, 4), lax.rem(step, 4)
        total = f32(m.cot[mic, :, lanes(block)])
        for offset, part in shifted(m.gpad, mic, block, 0, FRAMES):
            total = total + part * m.taps4[block, 31 - offset : 32 - offset]
        m.fgrad[mic, :, lanes(block)] = total.astype(bf16)
        return carry

    lax.fori_loop(0, 8, grad_block, 0)
    stores = [local(m.fgrad, frame_grad, m.store.at[1])]

    second = []
    for s in range(2):
        axis, axis2, _ = ORDERS[s]
        place = s * STREAM + getattr(here, axis) * FIRST
        for copy in first[s]:
            copy.wait_recv()
        part = rows_at(place, FIRST)
        total = f32(m.mine[part, :])
        for step in range(SIZES[axis] - 1):
            total = total + f32(m.rx1[s, step])
        m.mine[part, :] = total.astype(bf16)
        copies = []
        for step in (2, 1, 3):
            index, peer = here.along(axis2, step)
            copies.append(
                send(
                    m.mine.at[rows_at(place + index * SECOND, SECOND)],
                    m.rx2.at[s, step - 1],
                    m.s2.at[s, step - 1],
                    m.r2.at[s, step - 1],
                    peer,
                )
            )
        second.append((place, copies))
        sent += copies

    for copy in mixed_copies:
        copy.wait_recv()
    home_rows = m.mixed_home[...].reshape(2 * FRAMES, width)
    m.layer[...] = (
        f32(m.frames[...]) + dot(home_rows, m.w_out[...]).reshape(2, FRAMES, width)
    ).astype(bf16)
    stores.append(local(m.layer, layer_out, m.store.at[0]))

    block, part = tap_tile(here.z)
    total = m.tap0[block, part]
    for step in range(1, NZ):
        tap_copies[step - 1].wait_recv()
        total = total + m.tap_zrx[step - 1]

    def tap_axis(tile, axis, base):
        slot = base + getattr(here, axis)
        m.tap_rx[slot] = tile
        copies = []
        for step in range(1, SIZES[axis]):
            copies.append(
                send(
                    m.tap_rx.at[slot],
                    m.tap_rx.at[slot],
                    m.ts.at[NZ - 1 + base + step - 1],
                    m.tr.at[NZ - 1 + base + step - 1],
                    here.along(axis, step)[1],
                )
            )
        return copies

    def tap_sum(copies, base):
        for copy in copies:
            copy.wait_recv()
        total = m.tap_rx[base]
        for index in range(len(copies)):
            total = total + m.tap_rx[base + 1 + index]
        return total

    tap_x = tap_axis(total, "x", 0)
    sent += tap_x

    far_first = (4, 3, 5, 2, 6, 1, 7)
    third = []
    for s in range(2):
        axis2 = ORDERS[s][1]
        place, copies = second[s]
        place = place + getattr(here, axis2) * SECOND
        for copy in copies:
            copy.wait_recv()
        part = rows_at(place, SECOND)
        total = f32(m.mine[part, :])
        for step in range(SIZES[axis2] - 1):
            total = total + f32(m.rx2[s, step])
        m.mine[part, :] = total.astype(bf16)
        copies = []
        for step in far_first:
            index, peer = here.along("z", step)
            copies.append(
                send(
                    m.mine.at[rows_at(place + index * TILE, TILE)],
                    m.rx3.at[s, step - 1],
                    m.s3.at[s, step - 1],
                    m.r3.at[s, step - 1],
                    peer,
                )
            )
        third.append((place, copies))
        sent += copies

    tap_y = tap_axis(tap_sum(tap_x, 0), "y", 4)
    sent += tap_y

    def gather(s, level, axis, place, number):
        copies = {}
        base = (0, NZ - 1, NZ + 2)[level]
        part = rows_at(place, number)
        for step in far_first if level == 0 else (2, 1, 3):
            copies[step] = send(
                m.full.at[part],
                m.full.at[part],
                m.gs.at[s, base + step - 1],
                m.gr.at[s, base + step - 1],
                here.along(axis, step)[1],
            )
        return copies

    back = []
    for s in range(2):
        place, copies = third[s]
        for copy in copies:
            copy.wait_recv()
        part = rows_at(place + here.z * TILE, TILE)
        total = f32(m.mine[part, :])
        for step in range(NZ - 1):
            total = total + f32(m.rx3[s, step])
        m.full[part, :] = (total * scale).astype(bf16)
        copies = gather(s, 0, "z", place + here.z * TILE, TILE)
        back.append((place, copies))
        sent += copies.values()

    tap_c = tap_axis(tap_sum(tap_y, 4), "core", 8)
    sent += tap_c

    last = []

    def finished(s, slot, place):
        part, out = rows_at(place, FIRST), rows_at(core * HALF + place, FIRST)
        stores.append(local(m.full.at[part], grads_out.at[out], m.store.at[3 + s * 4 + slot]))
        last.append(
            send(
                m.full.at[part],
                grads_out.at[out],
                m.gcs.at[s, slot],
                m.gcr.at[s, slot],
                sibling,
            )
        )

    for level in (1, 2):
        for s in range(2):
            place, copies = back[s]
            for copy in copies.values():
                copy.wait_recv()
            axis = ORDERS[s][2 - level]
            number = (TILE, SECOND, FIRST)[level]
            copies = gather(s, level, axis, place, number)
            sent += copies.values()
            if level == 2:
                finished(s, 0, place)
            back[s] = (place - getattr(here, axis) * number, copies)
        if level == 1:
            block, part = tap_tile(here.z)
            m.tap_full[block, part] = tap_sum(tap_c, 8) * scale
            tap_back = []
            for step in far_first:
                tap_back.append(
                    send(
                        m.tap_full.at[block, part],
                        m.tap_full.at[block, part],
                        m.tgs.at[step - 1],
                        m.tgr.at[step - 1],
                        here.along("z", step)[1],
                    )
                )
            sent += tap_back
    for copy in tap_back:
        copy.wait_recv()
    for block in range(4):
        m.tap_sum[:, block * 128 : (block + 1) * 128] = m.tap_full[block, 0:31]
    stores.append(local(m.tap_sum, tap_out, m.store.at[2]))
    for copy in sent:
        copy.wait_send()
    for slot, step in enumerate((1, 3, 2)):
        for s in range(2):
            place, copies = back[s]
            copies[step].wait_recv()
            axis = ORDERS[s][0]
            size = SIZES[axis]
            index = lax.rem(getattr(here, axis) + size - step, size)
            finished(s, slot + 1, place + index * FIRST)
    for copy in stores:
        copy.wait()
    for copy in last:
        copy.wait_send()
        copy.wait_recv()


def memory(width):
    bf16, full = jnp.bfloat16, jnp.float32
    dma = pltpu.SemaphoreType.DMA
    rows = (8, SHARE, width)
    home = (2, FRAMES, width)
    wide = (2, 4, FRAMES + 32, 128)
    square = pltpu.VMEM((width, width), bf16)
    return dict(
        frames=pltpu.VMEM(home, bf16),
        cot=pltpu.VMEM(home, bf16),
        taps=pltpu.VMEM((31, width), full),
        w_query=square,
        w_key=square,
        w_value=square,
        w_out=square,
        layer=pltpu.VMEM(home, bf16),
        fgrad=pltpu.VMEM(home, bf16),
        tap_sum=pltpu.VMEM((31, width), full),
        halo=pltpu.VMEM((2, 2, 16, width), bf16),
        ghalo=pltpu.VMEM((2, 2, 16, width), bf16),
        ends=pltpu.VMEM((2, 2, 16, width), bf16),
        pool=pltpu.VMEM((10,) + rows, bf16),
        acted=pltpu.VMEM(home, bf16),
        taps4=pltpu.VMEM((4, 32, 128), full),
        fpad=pltpu.VMEM(wide, full),
        gpad=pltpu.VMEM(wide, full),
        dsilu=pltpu.VMEM((2, 4, FRAMES, 128), full),
        gather_heads=pltpu.VMEM((width, 128), bf16),
        spread_heads=pltpu.VMEM((128, width), bf16),
        queries=pltpu.VMEM(rows, bf16),
        keys=pltpu.VMEM(rows, bf16),
        values=pltpu.VMEM(rows, bf16),
        ups=pltpu.VMEM(rows, bf16),
        dkey=pltpu.VMEM(rows, full),
        dvalue=pltpu.VMEM(rows, full),
        dacted=pltpu.VMEM(rows, bf16),
        dacted_home=pltpu.VMEM(home, bf16),
        mixed_home=pltpu.VMEM(home, bf16),
        mine=pltpu.VMEM((HALF, 128), bf16),
        full=pltpu.VMEM((HALF, 128), bf16),
        rx1=pltpu.VMEM((2, 3, FIRST, 128), bf16),
        rx2=pltpu.VMEM((2, 3, SECOND, 128), bf16),
        rx3=pltpu.VMEM((2, NZ - 1, TILE, 128), bf16),
        tap0=pltpu.VMEM((4, 32, 128), full),
        tap_zrx=pltpu.VMEM((NZ - 1, 16, 128), full),
        tap_rx=pltpu.VMEM((10, 16, 128), full),
        tap_full=pltpu.VMEM((4, 32, 128), full),
        load=dma((7,)),
        store=dma((11,)),
        hs=dma((4,)),
        hr=dma((4,)),
        cs=dma((3,)),
        cr=dma((3,)),
        acs=dma((2, 3)),
        acr=dma((2, 3)),
        bs=dma((2, 3)),
        br=dma((2, 3)),
        core_s=dma((10,)),
        core_r=dma((10,)),
        s1=dma((2, 3)),
        r1=dma((2, 3)),
        s2=dma((2, 3)),
        r2=dma((2, 3)),
        s3=dma((2, NZ - 1)),
        r3=dma((2, NZ - 1)),
        gs=dma((2, NZ + 5)),
        gr=dma((2, NZ + 5)),
        gcs=dma((2, 4)),
        gcr=dma((2, 4)),
        ts=dma((NZ + 8,)),
        tr=dma((NZ + 8,)),
        tgs=dma((NZ - 1,)),
        tgr=dma((NZ - 1,)),
    )


def finish_body(layer, fgrad, taps, grads, layer_out, frame_grad, tap_out, *rest):
    outs, (packed, whole, held, held_taps, load, store) = rest[:4], rest[4:]
    loads = [local(grads.at[pl.ds(g * 2048, 2048)], packed.at[g], load.at[g]) for g in range(4)]
    small = ((layer, held.at[0], layer_out), (fgrad, held.at[1], frame_grad))
    small += ((taps, held_taps, tap_out),)
    first = [local(src, via, load.at[4 + at]) for at, (src, via, _) in enumerate(small)]
    moved = []
    for at, (_, via, dst) in enumerate(small):
        first[at].wait()
        moved.append(local(via, dst, store.at[4 + at]))
    for g in range(4):
        loads[g].wait()
        for block in range(4):
            whole[g, :, block * 128 : (block + 1) * 128] = f32(
                packed[g, block * 512 : (block + 1) * 512]
            )
        moved.append(local(whole.at[g], outs[g], store.at[g]))
    for copy in moved:
        copy.wait()


def shards(frames, cotangent, kernel, w_query, w_key, w_value, w_out):
    number, length, width = frames.shape
    scale = 1.0 / math.sqrt(lax.axis_size("mic") * number * lax.axis_size("tm") * length)
    scratch = memory(width)
    bf16, full = jnp.bfloat16, jnp.float32
    shape = jax.ShapeDtypeStruct
    outputs = (shape(frames.shape, bf16), shape(frames.shape, bf16), shape(kernel.shape, full))

    def body(*refs):
        parts = types.SimpleNamespace(**dict(zip(scratch, refs[11:])))
        kernel_body(scale, *refs[:11], parts)

    parts = pl.pallas_call(
        body,
        out_shape=outputs + (shape((2 * HALF, 128), bf16),),
        in_specs=[pl.BlockSpec(memory_space=pl.ANY)] * 7,
        out_specs=[pl.BlockSpec(memory_space=pl.ANY)] * 4,
        scratch_shapes=list(scratch.values()),
        compiler_params=pltpu.CompilerParams(
            collective_id=0, has_side_effects=True, vmem_limit_bytes=56 * 2**20
        ),
    )(frames, cotangent, kernel, w_query, w_key, w_value, w_out)
    dma = pltpu.SemaphoreType.DMA
    return pl.pallas_call(
        finish_body,
        out_shape=outputs + (shape((width, width), full),) * 4,
        in_specs=[pl.BlockSpec(memory_space=pl.ANY)] * 4,
        out_specs=[pl.BlockSpec(memory_space=pl.ANY)] * 7,
        scratch_shapes=[
            pltpu.VMEM((4, 2048, 128), bf16),
            pltpu.VMEM((4, width, width), full),
            pltpu.VMEM((2,) + frames.shape, bf16),
            pltpu.VMEM(kernel.shape, full),
            dma((7,)),
            dma((7,)),
        ],
        compiler_params=pltpu.CompilerParams(vmem_limit_bytes=56 * 2**20),
    )(*parts)


def solution(mesh):
    in_specs = (P("mic", "tm", None), P("mic", "tm", None), P(), P(), P(), P(), P())
    out_specs = (P("mic", "tm", None), P("mic", "tm", None), P(), P(), P(), P(), P())
    return jax.shard_map(shards, mesh=mesh, in_specs=in_specs, out_specs=out_specs, check_vma=False)
```

```python
import math
import types

import jax
import jax.numpy as jnp
from jax import lax
from jax.experimental import pallas as pl
from jax.experimental.pallas import tpu as pltpu
from jax.sharding import PartitionSpec as P

HEADS = 8
FRAMES = 128
SHARE = 32
NX, NY, NZ = 4, 4, 8
MESH = pl.DeviceIdType.MESH


class Place:
    def __init__(self):
        mic = lax.axis_index("mic")
        tm = lax.axis_index("tm")
        self.mic, self.tm = mic, tm
        self.core = lax.rem(mic, 2)
        self.x = lax.rem(tm, NX)
        self.z = lax.rem(lax.div(tm, NX), NZ)
        self.y = lax.div(tm, NX * NZ) * 2 + lax.div(mic, 2)

    def device(self, x=None, y=None, z=None, core=None):
        x = self.x if x is None else x
        y = self.y if y is None else y
        z = self.z if z is None else z
        core = self.core if core is None else core
        mic = lax.rem(y, 2) * 2 + core
        tm = lax.div(y, 2) * (NX * NZ) + z * NX + x
        return (mic, tm)

    def along(self, axis, step):
        size = {"x": NX, "y": NY, "z": NZ, "core": 2}[axis]
        index = lax.rem(getattr(self, axis) + step, size)
        return index, self.device(**{axis: index})


def rows_at(start, count):
    return pl.ds(pl.multiple_of(start, count), count)


def send(src, dst, send_sem, recv_sem, device):
    copy = pltpu.make_async_remote_copy(
        src_ref=src,
        dst_ref=dst,
        send_sem=send_sem,
        recv_sem=recv_sem,
        device_id=device,
        device_id_type=MESH,
    )
    copy.start()
    return copy


def local(src, dst, sem):
    copy = pltpu.make_async_copy(src, dst, sem)
    copy.start()
    return copy


SIZES = {"x": NX, "y": NY, "z": NZ, "core": 2}
SECOND, TILE = 128, 16
ORDERS = (("x", "y", "z"), ("y", "x", "z"))


ACT, ACT_S, MIXED, DQUERY, DKEY, DVALUE, COT, COT_S, FIRST_S, SECOND_S = range(10)


def f32(value):
    return value.astype(jnp.float32)


def dot(left, right, left_dim=1, right_dim=0):
    return lax.dot_general(
        left, right, (((left_dim,), (right_dim,)), ((), ())), preferred_element_type=jnp.float32
    )


def lanes(block):
    return pl.ds(pl.multiple_of(block * 128, 128), 128)


def shifted(padded, mic, block, base, count):
    for offset in range(1, 32):
        yield offset, padded[mic, block, base + offset : base + offset + count]


def kernel_body(
    scale,
    frames,
    cotangent,
    taps,
    w_query,
    w_key,
    w_value,
    w_out,
    layer_out,
    frame_grad,
    tap_out,
    grads_out,
    m,
):
    bf16 = jnp.bfloat16
    here = Place()
    width = frames.shape[2]
    rows = 8 * SHARE
    count = NX * NY * NZ // 2
    group = [lax.rem(here.mic + step, 4) for step in range(1, 4)]
    after = (here.mic, lax.rem(here.tm + 1, count))
    before = (here.mic, lax.rem(here.tm + count - 1, count))
    peers = [after, before]
    peers += [(mic, here.tm) for mic in group]
    for axis in ("core", "x", "y", "z"):
        for step in range(1, SIZES[axis]):
            peers.append(here.along(axis, step)[1])
    barrier = pltpu.get_barrier_semaphore()
    for peer in peers:
        pl.semaphore_signal(barrier, inc=1, device_id=peer, device_id_type=MESH)
    loads = {}
    for at, (name, source) in enumerate(
        (
            ("frames", frames),
            ("taps", taps),
            ("cot", cotangent),
            ("w_out", w_out),
            ("w_query", w_query),
            ("w_key", w_key),
            ("w_value", w_value),
        )
    ):
        loads[name] = local(source, getattr(m, name), m.load.at[at])
    pl.semaphore_wait(barrier, len(peers))
    sent = []

    halo = [
        send(frames.at[:, pl.ds(FRAMES - 16, 16), :], m.halo.at[0], m.hs.at[0], m.hr.at[0], after),
        send(frames.at[:, pl.ds(0, 16), :], m.halo.at[1], m.hs.at[1], m.hr.at[1], before),
    ]
    mics_here = pl.ds(here.mic * 2, 2)
    share_here = rows_at(here.mic * SHARE, SHARE)
    cot_copies = []
    for step, mic in enumerate(group):
        cot_copies.append(
            send(
                cotangent.at[:, rows_at(mic * SHARE, SHARE), :],
                m.pool.at[COT, mics_here],
                m.cs.at[step],
                m.cr.at[step],
                (mic, here.tm),
            )
        )
    sent += halo + cot_copies
    loads["frames"].wait()
    loads["taps"].wait()
    for block in range(4):
        m.taps4[block, 0:31] = m.taps[:, block * 128 : (block + 1) * 128]
        for mic in range(2):
            m.fpad[mic, block, 16 : 16 + FRAMES] = f32(
                m.frames[mic, :, block * 128 : (block + 1) * 128]
            )

    def conv_rows(mic, block, base, number):
        conv = jnp.zeros((number, 128), jnp.float32)
        for offset, part in shifted(m.fpad, mic, block, base, number):
            conv = conv + part * m.taps4[block, offset - 1 : offset]
        sig = 1.0 / (1.0 + jnp.exp(-conv))
        m.acted[mic, base : base + number, lanes(block)] = (conv * sig).astype(bf16)
        m.dsilu[mic, block, base : base + number] = sig * (1.0 + conv * (1.0 - sig))

    def inner_block(step, carry):
        conv_rows(lax.div(step, 4), lax.rem(step, 4), 16, FRAMES - 32)
        return carry

    lax.fori_loop(0, 8, inner_block, 0)

    row = lax.broadcasted_iota(jnp.int32, (512, 128), 0)
    col = lax.broadcasted_iota(jnp.int32, (512, 128), 1)
    m.gather_heads[...] = jnp.where(lax.div(row, 64) == col, 1.0, 0.0).astype(bf16)
    row = lax.broadcasted_iota(jnp.int32, (128, 512), 0)
    col = lax.broadcasted_iota(jnp.int32, (128, 512), 1)
    m.spread_heads[...] = jnp.where(lax.div(col, 64) == row, 1.0, 0.0).astype(bf16)
    loads["cot"].wait()
    m.pool[COT, mics_here] = m.cot[:, share_here, :]

    def fill_halo(side, pad, buffer, copy):
        copy.wait_recv()
        inside = here.tm > 0 if side == 0 else here.tm < count - 1
        place = slice(0, 16) if side == 0 else slice(16 + FRAMES, 32 + FRAMES)
        for mic in range(2):
            for block in range(4):
                value = f32(buffer[side, mic, :, block * 128 : (block + 1) * 128])
                pad[mic, block, place] = jnp.where(inside, value, 0.0)

    for side in range(2):
        fill_halo(side, m.fpad, m.halo, halo[side])

    act_copies = []
    for mic in range(2):

        def outer_block(block, carry):
            conv_rows(mic, block, 0, 16)
            conv_rows(mic, block, FRAMES - 16, 16)
            return carry

        lax.fori_loop(0, 4, outer_block, 0)
        for step, target in enumerate(group):
            act_copies.append(
                send(
                    m.acted.at[mic, rows_at(target * SHARE, SHARE), :],
                    m.pool.at[ACT, here.mic * 2 + mic],
                    m.acs.at[mic, step],
                    m.acr.at[mic, step],
                    (target, here.tm),
                )
            )
        m.pool[ACT, here.mic * 2 + mic] = m.acted[mic, share_here, :]
    sent += act_copies

    other, sibling = here.along("core", 1)

    def to_sibling(source, target):
        copy = send(
            m.pool.at[source],
            m.pool.at[target],
            m.core_s.at[target],
            m.core_r.at[target],
            sibling,
        )
        sent.append(copy)
        return copy

    for copy in cot_copies:
        copy.wait_recv()
    shared = {COT_S: to_sibling(COT, COT_S)}
    cot_rows = m.pool[COT].reshape(rows, width)
    loads["w_out"].wait()
    m.ups[...] = dot(cot_rows, m.w_out[...], 1, 1).astype(bf16).reshape(8, SHARE, width)
    for name in ("w_query", "w_key", "w_value"):
        loads[name].wait()
    for copy in act_copies:
        copy.wait_recv()
    shared[ACT_S] = to_sibling(ACT, ACT_S)
    act_rows = m.pool[ACT].reshape(rows, width)
    for weight, target in ((m.w_query, m.queries), (m.w_key, m.keys), (m.w_value, m.values)):
        target[...] = dot(act_rows, weight[...]).astype(bf16).reshape(8, SHARE, width)

    m.dkey[...] = jnp.zeros_like(m.dkey)
    m.dvalue[...] = jnp.zeros_like(m.dvalue)
    factor = 1.0 / math.sqrt(width // HEADS)

    def attend(index, carry):
        query, up = m.queries[index], m.ups[index]
        keys, values = m.keys[...], m.values[...]
        gather, spread = m.gather_heads[...], m.spread_heads[...]

        def per_head(product):
            return dot(product.reshape(rows, width), gather).reshape(8, SHARE, 128)

        def per_lane(heads):
            return dot(heads.astype(bf16).reshape(rows, 128), spread).reshape(8, SHARE, width)

        weights = jnp.exp(per_head(query[None] * keys) * factor)
        weights = weights / jnp.sum(weights, axis=0, keepdims=True)
        products = per_head(up[None] * values)
        inner = weights * (products - jnp.sum(weights * products, axis=0, keepdims=True)) * factor
        weights, inner = per_lane(weights), per_lane(inner)
        m.pool[MIXED, index] = jnp.sum(weights * f32(values), axis=0).astype(bf16)
        m.pool[DQUERY, index] = jnp.sum(inner * f32(keys), axis=0).astype(bf16)
        m.dkey[...] += inner * f32(query)[None]
        m.dvalue[...] += weights * f32(up)[None]
        return carry

    lax.fori_loop(0, 8, attend, 0)

    shared[FIRST_S] = to_sibling(DQUERY - other, FIRST_S)
    m.pool[DKEY] = m.dkey[...].astype(bf16)
    m.pool[DVALUE] = m.dvalue[...].astype(bf16)
    shared[SECOND_S] = to_sibling(DKEY + other, SECOND_S)

    def pooled(index):
        return m.pool[index].reshape(rows, width)

    dacted = dot(pooled(DQUERY), m.w_query[...], 1, 1)
    dacted = dacted + dot(pooled(DKEY), m.w_key[...], 1, 1)
    dacted = dacted + dot(pooled(DVALUE), m.w_value[...], 1, 1)
    m.dacted[...] = dacted.astype(bf16).reshape(8, SHARE, width)
    def send_home(kind, source, target):
        copies = []
        for step, mic in enumerate(group):
            copies.append(
                send(
                    source.at[pl.ds(mic * 2, 2)],
                    target.at[:, share_here, :],
                    m.bs.at[kind, step],
                    m.br.at[kind, step],
                    (mic, here.tm),
                )
            )
        target[:, share_here, :] = source[mics_here]
        sent.extend(copies)
        return copies

    dacted_copies = send_home(0, m.dacted, m.dacted_home)

    core = here.core
    operands = (
        ((ACT, DQUERY + 2 * core), (ACT_S, FIRST_S + core)),
        ((2 * core, DKEY + 2 * core), (ACT_S + 7 * core, SECOND_S - 2 * core)),
    )
    terms = []
    for mine, _ in operands:
        terms.append(dot(pooled(mine[0]), pooled(mine[1]), 0, 0))
    for copy in shared.values():
        copy.wait_recv()
    first = [{}, {}]
    for s in range(2):
        _, theirs = operands[s]
        term = (terms[s] + dot(pooled(theirs[0]), pooled(theirs[1]), 0, 0)).astype(bf16)
        for block in range(4):
            m.mine[s, block] = term[:, block * 128 : (block + 1) * 128].reshape(4, SECOND, 128)
        axis, axis2, _ = ORDERS[s]
        for far in (2, 1, 3, 0):
            index2, _ = here.along(axis2, far)
            for step in (2, 1, 3):
                index, peer = here.along(axis, step)
                first[s][far, step] = send(
                    m.mine.at[s, index, index2],
                    m.rx1.at[s, step - 1, far],
                    m.s1.at[s, step - 1, far],
                    m.r1.at[s, step - 1, far],
                    peer,
                )
        sent += first[s].values()

    for copy in dacted_copies:
        copy.wait_recv()

    def dconv_block(step, carry):
        mic, block = lax.div(step, 4), lax.rem(step, 4)
        dconv = f32(m.dacted_home[mic, :, lanes(block)]) * m.dsilu[mic, block]
        m.gpad[mic, block, 16 : 16 + FRAMES] = dconv
        m.ends[0, mic, :, lanes(block)] = dconv[FRAMES - 16 :].astype(bf16)
        m.ends[1, mic, :, lanes(block)] = dconv[:16].astype(bf16)
        return carry

    lax.fori_loop(0, 8, dconv_block, 0)
    ghalo = [
        send(m.ends.at[0], m.ghalo.at[0], m.hs.at[2], m.hr.at[2], after),
        send(m.ends.at[1], m.ghalo.at[1], m.hs.at[3], m.hr.at[3], before),
    ]
    sent += ghalo

    def tap_block(block, carry):
        sums = {}
        for mic in range(2):
            dconv = m.gpad[mic, block, 16 : 16 + FRAMES]
            for offset, part in shifted(m.fpad, mic, block, 0, FRAMES):
                part = jnp.sum((part * dconv).reshape(FRAMES // 8, 8, 128), axis=0)
                sums[offset] = sums[offset] + part if mic else part
        for offset, part in sums.items():
            m.tap0[block, offset - 1 : offset] = jnp.sum(part, axis=0, keepdims=True)
        m.tap0[block, 31:32] = jnp.zeros((1, 128), jnp.float32)
        return carry

    lax.fori_loop(0, 4, tap_block, 0)

    def tap_tile(index):
        return lax.div(index, 2), rows_at(lax.rem(index, 2) * 16, 16)

    tap_copies = []
    for step in range(1, NZ):
        index, peer = here.along("z", step)
        block, part = tap_tile(index)
        tap_copies.append(
            send(
                m.tap0.at[block, part],
                m.tap_zrx.at[step - 1],
                m.ts.at[step - 1],
                m.tr.at[step - 1],
                peer,
            )
        )
    sent += tap_copies

    second = [{}, {}]
    for far in (2, 1, 3, 0):
        for s in range(2):
            axis, axis2, _ = ORDERS[s]
            index = getattr(here, axis)
            index2, peer = here.along(axis2, far)
            total = f32(m.mine[s, index, index2])
            for step in (1, 2, 3):
                first[s][far, step].wait_recv()
                total = total + f32(m.rx1[s, step - 1, far])
            m.mine[s, index, index2] = total.astype(bf16)
            if far:
                second[s][far] = send(
                    m.mine.at[s, index, index2],
                    m.rx2.at[s, far - 1],
                    m.s2.at[s, far - 1],
                    m.r2.at[s, far - 1],
                    peer,
                )
                sent.append(second[s][far])

    block, part = tap_tile(here.z)
    total = m.tap0[block, part]
    for step in range(1, NZ):
        tap_copies[step - 1].wait_recv()
        total = total + m.tap_zrx[step - 1]

    def tap_axis(tile, axis, base):
        slot = base + getattr(here, axis)
        m.tap_rx[slot] = tile
        copies = []
        for step in range(1, SIZES[axis]):
            copies.append(
                send(
                    m.tap_rx.at[slot],
                    m.tap_rx.at[slot],
                    m.ts.at[NZ - 1 + base + step - 1],
                    m.tr.at[NZ - 1 + base + step - 1],
                    here.along(axis, step)[1],
                )
            )
        return copies

    def tap_sum(copies, base):
        for copy in copies:
            copy.wait_recv()
        total = m.tap_rx[base]
        for index in range(len(copies)):
            total = total + m.tap_rx[base + 1 + index]
        return total

    tap_x = tap_axis(total, "x", 0)
    sent += tap_x

    for side in range(2):
        fill_halo(side, m.gpad, m.ghalo, ghalo[side])

    def grad_block(step, carry):
        mic, block = lax.div(step, 4), lax.rem(step, 4)
        total = f32(m.cot[mic, :, lanes(block)])
        for offset, part in shifted(m.gpad, mic, block, 0, FRAMES):
            total = total + part * m.taps4[block, 31 - offset : 32 - offset]
        m.fgrad[mic, :, lanes(block)] = total.astype(bf16)
        return carry

    lax.fori_loop(0, 8, grad_block, 0)
    stores = [local(m.fgrad, frame_grad, m.store.at[1])]

    far_first = (4, 3, 5, 2, 6, 1, 7)
    third = []
    for s in range(2):
        axis, axis2, _ = ORDERS[s]
        block = (s, getattr(here, axis), getattr(here, axis2))
        total = f32(m.mine[block])
        for far in (1, 2, 3):
            second[s][far].wait_recv()
            total = total + f32(m.rx2[s, far - 1])
        m.mine[block] = total.astype(bf16)
        copies = []
        for step in far_first:
            index, peer = here.along("z", step)
            copies.append(
                send(
                    m.mine.at[block + (rows_at(index * TILE, TILE),)],
                    m.rx3.at[s, step - 1],
                    m.s3.at[s, step - 1],
                    m.r3.at[s, step - 1],
                    peer,
                )
            )
        third.append((block, copies))
        sent += copies
    mixed_copies = send_home(1, m.pool.at[MIXED], m.mixed_home)

    tap_y = tap_axis(tap_sum(tap_x, 0), "y", 4)
    sent += tap_y

    back = []
    for s in range(2):
        block, copies = third[s]
        part = block + (rows_at(here.z * TILE, TILE),)
        total = f32(m.mine[part])
        for copy in copies:
            copy.wait_recv()
        for step in range(NZ - 1):
            total = total + f32(m.rx3[s, step])
        m.full[part] = (total * scale).astype(bf16)
        copies = []
        for step in far_first:
            copies.append(
                send(
                    m.full.at[part],
                    m.full.at[part],
                    m.gs.at[s, step - 1],
                    m.gr.at[s, step - 1],
                    here.along("z", step)[1],
                )
            )
        back.append(copies)
        sent += copies

    tap_c = tap_axis(tap_sum(tap_y, 4), "core", 8)
    sent += tap_c

    for copy in mixed_copies:
        copy.wait_recv()
    home_rows = m.mixed_home[...].reshape(2 * FRAMES, width)
    m.layer[...] = (
        f32(m.frames[...]) + dot(home_rows, m.w_out[...]).reshape(2, FRAMES, width)
    ).astype(bf16)
    stores.append(local(m.layer, layer_out, m.store.at[0]))

    block, part = tap_tile(here.z)
    m.tap_full[block, part] = tap_sum(tap_c, 8) * scale
    tap_back = []
    for step in far_first:
        tap_back.append(
            send(
                m.tap_full.at[block, part],
                m.tap_full.at[block, part],
                m.tgs.at[step - 1],
                m.tgr.at[step - 1],
                here.along("z", step)[1],
            )
        )
    sent += tap_back

    def pass_on(s, axis, block, kind):
        copies = []
        for step in (2, 1, 3):
            copies.append(
                send(
                    m.full.at[block],
                    m.full.at[block],
                    m.gs.at[s, NZ - 1 + kind * 3 + step - 1],
                    m.gr.at[s, NZ - 1 + kind * 3 + step - 1],
                    here.along(axis, step)[1],
                )
            )
        sent.extend(copies)
        return copies

    across, along = [], [{}, {}]
    for s in range(2):
        for copy in back[s]:
            copy.wait_recv()
        block, _ = third[s]
        across.append(pass_on(s, ORDERS[s][1], block, 0))
        along[s][0] = pass_on(s, ORDERS[s][0], block, 1)

    def sender(axis, step):
        return lax.rem(getattr(here, axis) + SIZES[axis] - step, SIZES[axis])

    for at, step in ((1, 1), (2, 3), (0, 2)):
        for s in range(2):
            axis, axis2, _ = ORDERS[s]
            across[s][at].wait_recv()
            block = (s, getattr(here, axis), sender(axis2, step))
            along[s][step] = pass_on(s, axis, block, 1 + step)
    for copy in tap_back:
        copy.wait_recv()
    for block in range(4):
        m.tap_sum[:, block * 128 : (block + 1) * 128] = m.tap_full[block, 0:31]
    stores.append(local(m.tap_sum, tap_out, m.store.at[2]))
    for copy in sent:
        copy.wait_send()
    last = []
    for step in (0, 1, 3, 2):
        for s in range(2):
            for copy in along[s][step]:
                copy.wait_recv()
            index2 = sender(ORDERS[s][1], step)
            source = m.full.at[s, :, index2]
            target = grads_out.at[core, s, :, index2]
            stores.append(local(source, target, m.store.at[3 + s * 4 + step]))
            last.append(send(source, target, m.gcs.at[s, step], m.gcr.at[s, step], sibling))
    for copy in stores:
        copy.wait()
    for copy in last:
        copy.wait_send()
        copy.wait_recv()


def memory(width):
    bf16, full = jnp.bfloat16, jnp.float32
    dma = pltpu.SemaphoreType.DMA
    rows = (8, SHARE, width)
    home = (2, FRAMES, width)
    wide = (2, 4, FRAMES + 32, 128)
    square = pltpu.VMEM((width, width), bf16)
    return dict(
        frames=pltpu.VMEM(home, bf16),
        cot=pltpu.VMEM(home, bf16),
        taps=pltpu.VMEM((31, width), full),
        w_query=square,
        w_key=square,
        w_value=square,
        w_out=square,
        layer=pltpu.VMEM(home, bf16),
        fgrad=pltpu.VMEM(home, bf16),
        tap_sum=pltpu.VMEM((31, width), full),
        halo=pltpu.VMEM((2, 2, 16, width), bf16),
        ghalo=pltpu.VMEM((2, 2, 16, width), bf16),
        ends=pltpu.VMEM((2, 2, 16, width), bf16),
        pool=pltpu.VMEM((10,) + rows, bf16),
        acted=pltpu.VMEM(home, bf16),
        taps4=pltpu.VMEM((4, 32, 128), full),
        fpad=pltpu.VMEM(wide, full),
        gpad=pltpu.VMEM(wide, full),
        dsilu=pltpu.VMEM((2, 4, FRAMES, 128), full),
        gather_heads=pltpu.VMEM((width, 128), bf16),
        spread_heads=pltpu.VMEM((128, width), bf16),
        queries=pltpu.VMEM(rows, bf16),
        keys=pltpu.VMEM(rows, bf16),
        values=pltpu.VMEM(rows, bf16),
        ups=pltpu.VMEM(rows, bf16),
        dkey=pltpu.VMEM(rows, full),
        dvalue=pltpu.VMEM(rows, full),
        dacted=pltpu.VMEM(rows, bf16),
        dacted_home=pltpu.VMEM(home, bf16),
        mixed_home=pltpu.VMEM(home, bf16),
        mine=pltpu.VMEM((2, 4, 4, SECOND, 128), bf16),
        full=pltpu.VMEM((2, 4, 4, SECOND, 128), bf16),
        rx1=pltpu.VMEM((2, 3, 4, SECOND, 128), bf16),
        rx2=pltpu.VMEM((2, 3, SECOND, 128), bf16),
        rx3=pltpu.VMEM((2, NZ - 1, TILE, 128), bf16),
        tap0=pltpu.VMEM((4, 32, 128), full),
        tap_zrx=pltpu.VMEM((NZ - 1, 16, 128), full),
        tap_rx=pltpu.VMEM((10, 16, 128), full),
        tap_full=pltpu.VMEM((4, 32, 128), full),
        load=dma((7,)),
        store=dma((11,)),
        hs=dma((4,)),
        hr=dma((4,)),
        cs=dma((3,)),
        cr=dma((3,)),
        acs=dma((2, 3)),
        acr=dma((2, 3)),
        bs=dma((2, 3)),
        br=dma((2, 3)),
        core_s=dma((10,)),
        core_r=dma((10,)),
        s1=dma((2, 3, 4)),
        r1=dma((2, 3, 4)),
        s2=dma((2, 3)),
        r2=dma((2, 3)),
        s3=dma((2, NZ - 1)),
        r3=dma((2, NZ - 1)),
        gs=dma((2, NZ + 14)),
        gr=dma((2, NZ + 14)),
        gcs=dma((2, 4)),
        gcr=dma((2, 4)),
        ts=dma((NZ + 8,)),
        tr=dma((NZ + 8,)),
        tgs=dma((NZ - 1,)),
        tgr=dma((NZ - 1,)),
    )


def finish_body(layer, fgrad, taps, grads, layer_out, frame_grad, tap_out, *rest):
    outs, (packed, whole, held, held_taps, load, store) = rest[:4], rest[4:]
    chunks = [(g, half) for g in range(4) for half in range(2)]
    loads = []
    for at, (g, half) in enumerate(chunks):
        part = grads.at[g // 2, g % 2, :, pl.ds(half * 2, 2)]
        loads.append(local(part, packed.at[g, half], load.at[at]))
    small = ((layer, held.at[0], layer_out), (fgrad, held.at[1], frame_grad))
    small += ((taps, held_taps, tap_out),)
    first = [local(src, via, load.at[8 + at]) for at, (src, via, _) in enumerate(small)]
    moved = []
    for at, (g, half) in enumerate(chunks):
        loads[at].wait()
        rows = pl.ds(half * 256, 256)
        for block in range(4):
            value = f32(packed[g, half, block]).reshape(256, 128)
            whole[g, rows, block * 128 : (block + 1) * 128] = value
        moved.append(local(whole.at[g, rows], outs[g].at[rows], store.at[at]))
    for at, (_, via, dst) in enumerate(small):
        first[at].wait()
        moved.append(local(via, dst, store.at[8 + at]))
    for copy in moved:
        copy.wait()


def shards(frames, cotangent, kernel, w_query, w_key, w_value, w_out):
    number, length, width = frames.shape
    scale = 1.0 / math.sqrt(lax.axis_size("mic") * number * lax.axis_size("tm") * length)
    scratch = memory(width)
    bf16, full = jnp.bfloat16, jnp.float32
    shape = jax.ShapeDtypeStruct
    outputs = (shape(frames.shape, bf16), shape(frames.shape, bf16), shape(kernel.shape, full))

    def body(*refs):
        parts = types.SimpleNamespace(**dict(zip(scratch, refs[11:])))
        kernel_body(scale, *refs[:11], parts)

    parts = pl.pallas_call(
        body,
        out_shape=outputs + (shape((2, 2, 4, 4, SECOND, 128), bf16),),
        in_specs=[pl.BlockSpec(memory_space=pl.ANY)] * 7,
        out_specs=[pl.BlockSpec(memory_space=pl.ANY)] * 4,
        scratch_shapes=list(scratch.values()),
        compiler_params=pltpu.CompilerParams(
            collective_id=0, has_side_effects=True, vmem_limit_bytes=56 * 2**20
        ),
    )(frames, cotangent, kernel, w_query, w_key, w_value, w_out)
    dma = pltpu.SemaphoreType.DMA
    return pl.pallas_call(
        finish_body,
        out_shape=outputs + (shape((width, width), full),) * 4,
        in_specs=[pl.BlockSpec(memory_space=pl.ANY)] * 4,
        out_specs=[pl.BlockSpec(memory_space=pl.ANY)] * 7,
        scratch_shapes=[
            pltpu.VMEM((4, 2, 4, 2, SECOND, 128), bf16),
            pltpu.VMEM((4, width, width), full),
            pltpu.VMEM((2,) + frames.shape, bf16),
            pltpu.VMEM(kernel.shape, full),
            dma((11,)),
            dma((11,)),
        ],
        compiler_params=pltpu.CompilerParams(vmem_limit_bytes=56 * 2**20),
    )(*parts)


def solution(mesh):
    in_specs = (P("mic", "tm", None), P("mic", "tm", None), P(), P(), P(), P(), P())
    out_specs = (P("mic", "tm", None), P("mic", "tm", None), P(), P(), P(), P(), P())
    return jax.shard_map(shards, mesh=mesh, in_specs=in_specs, out_specs=out_specs, check_vma=False)
```

```python
import math
import types

import jax
import jax.numpy as jnp
from jax import lax
from jax.experimental import pallas as pl
from jax.experimental.pallas import tpu as pltpu
from jax.sharding import PartitionSpec as P

HEADS = 8
FRAMES = 128
SHARE = 32
NX, NY, NZ = 4, 4, 8
MESH = pl.DeviceIdType.MESH


class Place:
    def __init__(self):
        mic = lax.axis_index("mic")
        tm = lax.axis_index("tm")
        self.mic, self.tm = mic, tm
        self.core = lax.rem(mic, 2)
        self.x = lax.rem(tm, NX)
        self.z = lax.rem(lax.div(tm, NX), NZ)
        self.y = lax.div(tm, NX * NZ) * 2 + lax.div(mic, 2)

    def device(self, x=None, y=None, z=None, core=None):
        x = self.x if x is None else x
        y = self.y if y is None else y
        z = self.z if z is None else z
        core = self.core if core is None else core
        mic = lax.rem(y, 2) * 2 + core
        tm = lax.div(y, 2) * (NX * NZ) + z * NX + x
        return (mic, tm)

    def along(self, axis, step):
        size = {"x": NX, "y": NY, "z": NZ, "core": 2}[axis]
        index = lax.rem(getattr(self, axis) + step, size)
        return index, self.device(**{axis: index})


def rows_at(start, count):
    return pl.ds(pl.multiple_of(start, count), count)


def send(src, dst, send_sem, recv_sem, device):
    copy = pltpu.make_async_remote_copy(
        src_ref=src,
        dst_ref=dst,
        send_sem=send_sem,
        recv_sem=recv_sem,
        device_id=device,
        device_id_type=MESH,
    )
    copy.start()
    return copy


def local(src, dst, sem):
    copy = pltpu.make_async_copy(src, dst, sem)
    copy.start()
    return copy


SIZES = {"x": NX, "y": NY, "z": NZ, "core": 2}
SECOND, TILE = 128, 16
ORDERS = (("x", "y", "z"), ("y", "x", "z"))


ACT, ACT_S, MIXED, DQUERY, DKEY, DVALUE, COT, COT_S, FIRST_S, SECOND_S = range(10)


def f32(value):
    return value.astype(jnp.float32)


def dot(left, right, left_dim=1, right_dim=0):
    return lax.dot_general(
        left, right, (((left_dim,), (right_dim,)), ((), ())), preferred_element_type=jnp.float32
    )


def lanes(block):
    return pl.ds(pl.multiple_of(block * 128, 128), 128)


def shifted(padded, mic, block, base, count):
    for offset in range(1, 32):
        yield offset, padded[mic, block, base + offset : base + offset + count]


def kernel_body(
    scale,
    frames,
    cotangent,
    taps,
    w_query,
    w_key,
    w_value,
    w_out,
    layer_out,
    frame_grad,
    tap_out,
    grads_out,
    m,
):
    bf16 = jnp.bfloat16
    here = Place()
    width = frames.shape[2]
    rows = 8 * SHARE
    count = NX * NY * NZ // 2
    group = [lax.rem(here.mic + step, 4) for step in range(1, 4)]
    after = (here.mic, lax.rem(here.tm + 1, count))
    before = (here.mic, lax.rem(here.tm + count - 1, count))
    peers = [after, before]
    peers += [(mic, here.tm) for mic in group]
    for axis in ("core", "x", "y", "z"):
        for step in range(1, SIZES[axis]):
            peers.append(here.along(axis, step)[1])
    over = [lax.rem(here.x + step, NX) for step in range(1, NX)]
    peers += [here.device(x=x, core=1 - here.core) for x in over]
    barrier = pltpu.get_barrier_semaphore()
    for peer in peers:
        pl.semaphore_signal(barrier, inc=1, device_id=peer, device_id_type=MESH)
    loads = {}
    for at, (name, source) in enumerate(
        (
            ("frames", frames),
            ("taps", taps),
            ("cot", cotangent),
            ("w_out", w_out),
            ("w_query", w_query),
            ("w_key", w_key),
            ("w_value", w_value),
        )
    ):
        loads[name] = local(source, getattr(m, name), m.load.at[at])
    pl.semaphore_wait(barrier, len(peers))
    sent = []

    halo = [
        send(frames.at[:, pl.ds(FRAMES - 16, 16), :], m.halo.at[0], m.hs.at[0], m.hr.at[0], after),
        send(frames.at[:, pl.ds(0, 16), :], m.halo.at[1], m.hs.at[1], m.hr.at[1], before),
    ]
    mics_here = pl.ds(here.mic * 2, 2)
    share_here = rows_at(here.mic * SHARE, SHARE)
    cot_copies = []
    for step, mic in enumerate(group):
        cot_copies.append(
            send(
                cotangent.at[:, rows_at(mic * SHARE, SHARE), :],
                m.pool.at[COT, mics_here],
                m.cs.at[step],
                m.cr.at[step],
                (mic, here.tm),
            )
        )
    sent += halo + cot_copies
    loads["frames"].wait()
    loads["taps"].wait()
    for block in range(4):
        m.taps4[block, 0:31] = m.taps[:, block * 128 : (block + 1) * 128]
        for mic in range(2):
            m.fpad[mic, block, 16 : 16 + FRAMES] = f32(
                m.frames[mic, :, block * 128 : (block + 1) * 128]
            )

    def conv_rows(mic, block, base, number):
        conv = jnp.zeros((number, 128), jnp.float32)
        for offset, part in shifted(m.fpad, mic, block, base, number):
            conv = conv + part * m.taps4[block, offset - 1 : offset]
        sig = 1.0 / (1.0 + jnp.exp(-conv))
        m.acted[mic, base : base + number, lanes(block)] = (conv * sig).astype(bf16)
        m.dsilu[mic, block, base : base + number] = sig * (1.0 + conv * (1.0 - sig))

    def inner_block(step, carry):
        conv_rows(lax.div(step, 4), lax.rem(step, 4), 16, FRAMES - 32)
        return carry

    lax.fori_loop(0, 8, inner_block, 0)

    row = lax.broadcasted_iota(jnp.int32, (512, 128), 0)
    col = lax.broadcasted_iota(jnp.int32, (512, 128), 1)
    m.gather_heads[...] = jnp.where(lax.div(row, 64) == col, 1.0, 0.0).astype(bf16)
    row = lax.broadcasted_iota(jnp.int32, (128, 512), 0)
    col = lax.broadcasted_iota(jnp.int32, (128, 512), 1)
    m.spread_heads[...] = jnp.where(lax.div(col, 64) == row, 1.0, 0.0).astype(bf16)
    loads["cot"].wait()
    m.pool[COT, mics_here] = m.cot[:, share_here, :]

    def fill_halo(side, pad, buffer, copy):
        copy.wait_recv()
        inside = here.tm > 0 if side == 0 else here.tm < count - 1
        place = slice(0, 16) if side == 0 else slice(16 + FRAMES, 32 + FRAMES)
        for mic in range(2):
            for block in range(4):
                value = f32(buffer[side, mic, :, block * 128 : (block + 1) * 128])
                pad[mic, block, place] = jnp.where(inside, value, 0.0)

    for side in range(2):
        fill_halo(side, m.fpad, m.halo, halo[side])

    act_copies = []
    for mic in range(2):

        def outer_block(block, carry):
            conv_rows(mic, block, 0, 16)
            conv_rows(mic, block, FRAMES - 16, 16)
            return carry

        lax.fori_loop(0, 4, outer_block, 0)
        for step, target in enumerate(group):
            act_copies.append(
                send(
                    m.acted.at[mic, rows_at(target * SHARE, SHARE), :],
                    m.pool.at[ACT, here.mic * 2 + mic],
                    m.acs.at[mic, step],
                    m.acr.at[mic, step],
                    (target, here.tm),
                )
            )
        m.pool[ACT, here.mic * 2 + mic] = m.acted[mic, share_here, :]
    sent += act_copies

    other, sibling = here.along("core", 1)

    def to_sibling(source, target):
        copy = send(
            m.pool.at[source],
            m.pool.at[target],
            m.core_s.at[target],
            m.core_r.at[target],
            sibling,
        )
        sent.append(copy)
        return copy

    for copy in cot_copies:
        copy.wait_recv()
    shared = {COT_S: to_sibling(COT, COT_S)}
    cot_rows = m.pool[COT].reshape(rows, width)
    loads["w_out"].wait()
    m.ups[...] = dot(cot_rows, m.w_out[...], 1, 1).astype(bf16).reshape(8, SHARE, width)
    for name in ("w_query", "w_key", "w_value"):
        loads[name].wait()
    for copy in act_copies:
        copy.wait_recv()
    shared[ACT_S] = to_sibling(ACT, ACT_S)
    act_rows = m.pool[ACT].reshape(rows, width)
    for weight, target in ((m.w_query, m.queries), (m.w_key, m.keys), (m.w_value, m.values)):
        target[...] = dot(act_rows, weight[...]).astype(bf16).reshape(8, SHARE, width)

    factor = 1.0 / math.sqrt(width // HEADS)

    def attend(index):
        query, up = m.queries[index], m.ups[index]
        keys, values = m.keys[...], m.values[...]
        gather, spread = m.gather_heads[...], m.spread_heads[...]

        def per_head(product):
            return dot(product.reshape(rows, width), gather).reshape(8, SHARE, 128)

        def per_lane(heads):
            return dot(heads.astype(bf16).reshape(rows, 128), spread).reshape(8, SHARE, width)

        weights = jnp.exp(per_head(query[None] * keys) * factor)
        weights = weights / jnp.sum(weights, axis=0, keepdims=True)
        products = per_head(up[None] * values)
        inner = weights * (products - jnp.sum(weights * products, axis=0, keepdims=True)) * factor
        weights, inner = per_lane(weights), per_lane(inner)
        m.pool[MIXED, index] = jnp.sum(weights * f32(values), axis=0).astype(bf16)
        m.pool[DQUERY, index] = jnp.sum(inner * f32(keys), axis=0).astype(bf16)
        return inner * f32(query)[None], weights * f32(up)[None]

    def attend_two(step, carry):
        dkey, dvalue = attend(2 * step)
        dkey_too, dvalue_too = attend(2 * step + 1)
        dkey, dvalue = dkey + dkey_too, dvalue + dvalue_too

        @pl.when(step == 0)
        def _():
            m.dkey[...] = dkey
            m.dvalue[...] = dvalue

        @pl.when(step > 0)
        def _():
            m.dkey[...] += dkey
            m.dvalue[...] += dvalue

        return carry

    lax.fori_loop(0, 4, attend_two, 0)

    shared[FIRST_S] = to_sibling(DQUERY - other, FIRST_S)
    m.pool[DKEY] = m.dkey[...].astype(bf16)
    m.pool[DVALUE] = m.dvalue[...].astype(bf16)
    shared[SECOND_S] = to_sibling(DKEY + other, SECOND_S)

    def pooled(index):
        return m.pool[index].reshape(rows, width)

    dacted = dot(pooled(DQUERY), m.w_query[...], 1, 1)
    dacted = dacted + dot(pooled(DKEY), m.w_key[...], 1, 1)
    dacted = dacted + dot(pooled(DVALUE), m.w_value[...], 1, 1)
    m.dacted[...] = dacted.astype(bf16).reshape(8, SHARE, width)
    def send_home(kind, source, target):
        copies = []
        for step, mic in enumerate(group):
            copies.append(
                send(
                    source.at[pl.ds(mic * 2, 2)],
                    target.at[:, share_here, :],
                    m.bs.at[kind, step],
                    m.br.at[kind, step],
                    (mic, here.tm),
                )
            )
        target[:, share_here, :] = source[mics_here]
        sent.extend(copies)
        return copies

    dacted_copies = send_home(0, m.dacted, m.dacted_home)

    core = here.core
    operands = (
        ((ACT, DQUERY + 2 * core), (ACT_S, FIRST_S + core)),
        ((2 * core, DKEY + 2 * core), (ACT_S + 7 * core, SECOND_S - 2 * core)),
    )
    terms = []
    for mine, _ in operands:
        terms.append(dot(pooled(mine[0]), pooled(mine[1]), 0, 0))
    for copy in shared.values():
        copy.wait_recv()
    first = [{}, {}]
    for s in range(2):
        _, theirs = operands[s]
        term = (terms[s] + dot(pooled(theirs[0]), pooled(theirs[1]), 0, 0)).astype(bf16)
        for block in range(4):
            m.mine[s, block] = term[:, block * 128 : (block + 1) * 128].reshape(4, SECOND, 128)
        axis, axis2, _ = ORDERS[s]
        for far in (2, 1, 3, 0):
            index2, _ = here.along(axis2, far)
            for step in (2, 1, 3):
                index, peer = here.along(axis, step)
                first[s][far, step] = send(
                    m.mine.at[s, index, index2],
                    m.rx1.at[s, step - 1, far],
                    m.s1.at[s, step - 1, far],
                    m.r1.at[s, step - 1, far],
                    peer,
                )
        sent += first[s].values()

    for copy in dacted_copies:
        copy.wait_recv()

    def dconv_block(step, carry):
        mic, block = lax.div(step, 4), lax.rem(step, 4)
        dconv = f32(m.dacted_home[mic, :, lanes(block)]) * m.dsilu[mic, block]
        m.gpad[mic, block, 16 : 16 + FRAMES] = dconv
        m.ends[0, mic, :, lanes(block)] = dconv[FRAMES - 16 :].astype(bf16)
        m.ends[1, mic, :, lanes(block)] = dconv[:16].astype(bf16)
        return carry

    lax.fori_loop(0, 8, dconv_block, 0)
    ghalo = [
        send(m.ends.at[0], m.ghalo.at[0], m.hs.at[2], m.hr.at[2], after),
        send(m.ends.at[1], m.ghalo.at[1], m.hs.at[3], m.hr.at[3], before),
    ]
    sent += ghalo

    def tap_block(block, carry):
        sums = {}
        for mic in range(2):
            dconv = m.gpad[mic, block, 16 : 16 + FRAMES]
            for offset, part in shifted(m.fpad, mic, block, 0, FRAMES):
                part = jnp.sum((part * dconv).reshape(FRAMES // 8, 8, 128), axis=0)
                sums[offset] = sums[offset] + part if mic else part
        for offset, part in sums.items():
            m.tap0[block, offset - 1 : offset] = jnp.sum(part, axis=0, keepdims=True)
        m.tap0[block, 31:32] = jnp.zeros((1, 128), jnp.float32)
        return carry

    lax.fori_loop(0, 4, tap_block, 0)

    def tap_tile(index):
        return lax.div(index, 2), rows_at(lax.rem(index, 2) * 16, 16)

    tap_copies = []
    for step in range(1, NZ):
        index, peer = here.along("z", step)
        block, part = tap_tile(index)
        tap_copies.append(
            send(
                m.tap0.at[block, part],
                m.tap_zrx.at[step - 1],
                m.ts.at[step - 1],
                m.tr.at[step - 1],
                peer,
            )
        )
    sent += tap_copies

    second = [{}, {}]
    for far in (2, 1, 3, 0):
        for s in range(2):
            axis, axis2, _ = ORDERS[s]
            index = getattr(here, axis)
            index2, peer = here.along(axis2, far)
            total = f32(m.mine[s, index, index2])
            for step in (1, 2, 3):
                first[s][far, step].wait_recv()
                total = total + f32(m.rx1[s, step - 1, far])
            m.mine[s, index, index2] = total.astype(bf16)
            if far:
                second[s][far] = send(
                    m.mine.at[s, index, index2],
                    m.rx2.at[s, far - 1],
                    m.s2.at[s, far - 1],
                    m.r2.at[s, far - 1],
                    peer,
                )
                sent.append(second[s][far])

    far_first = (4, 3, 5, 2, 6, 1, 7)
    third = []
    for s in range(2):
        axis, axis2, _ = ORDERS[s]
        block = (s, getattr(here, axis), getattr(here, axis2))
        total = f32(m.mine[block])
        for far in (1, 2, 3):
            second[s][far].wait_recv()
            total = total + f32(m.rx2[s, far - 1])
        m.mine[block] = total.astype(bf16)
        copies = []
        for step in far_first:
            index, peer = here.along("z", step)
            copies.append(
                send(
                    m.mine.at[block + (rows_at(index * TILE, TILE),)],
                    m.rx3.at[s, step - 1],
                    m.s3.at[s, step - 1],
                    m.r3.at[s, step - 1],
                    peer,
                )
            )
        third.append((block, copies))
        sent += copies
    mixed_copies = send_home(1, m.pool.at[MIXED], m.mixed_home)

    for side in range(2):
        fill_halo(side, m.gpad, m.ghalo, ghalo[side])

    def grad_block(step, carry):
        mic, block = lax.div(step, 4), lax.rem(step, 4)
        total = f32(m.cot[mic, :, lanes(block)])
        for offset, part in shifted(m.gpad, mic, block, 0, FRAMES):
            total = total + part * m.taps4[block, 31 - offset : 32 - offset]
        m.fgrad[mic, :, lanes(block)] = total.astype(bf16)
        return carry

    lax.fori_loop(0, 8, grad_block, 0)
    stores = [local(m.fgrad, frame_grad, m.store.at[1])]

    block, part = tap_tile(here.z)
    total = m.tap0[block, part]
    for step in range(1, NZ):
        tap_copies[step - 1].wait_recv()
        total = total + m.tap_zrx[step - 1]

    def tap_share(tile, slot, base, others):
        m.tap_rx[slot] = tile
        copies = []
        for at, peer in enumerate(others):
            copies.append(
                send(m.tap_rx.at[slot], m.tap_rx.at[slot], m.ts.at[base + at], m.tr.at[base + at], peer)
            )
        return copies

    def tap_sum(copies, base):
        for copy in copies:
            copy.wait_recv()
        total = m.tap_rx[base]
        for index in range(len(copies)):
            total = total + m.tap_rx[base + 1 + index]
        return total

    others = [here.device(x=x, core=core) for x in over for core in (here.core, 1 - here.core)]
    others.append(sibling)
    tap_x = tap_share(total, here.x * 2 + here.core, NZ - 1, others)
    sent += tap_x

    back = []
    for s in range(2):
        block, copies = third[s]
        part = block + (rows_at(here.z * TILE, TILE),)
        total = f32(m.mine[part])
        for copy in copies:
            copy.wait_recv()
        for step in range(NZ - 1):
            total = total + f32(m.rx3[s, step])
        m.full[part] = (total * scale).astype(bf16)
        copies = []
        for step in far_first:
            copies.append(
                send(
                    m.full.at[part],
                    m.full.at[part],
                    m.gs.at[s, step - 1],
                    m.gr.at[s, step - 1],
                    here.along("z", step)[1],
                )
            )
        back.append(copies)
        sent += copies

    others = [here.along("y", step)[1] for step in (2, 1, 3)]
    tap_y = tap_share(tap_sum(tap_x, 0), 8 + here.y, NZ + 6, others)
    sent += tap_y

    for copy in mixed_copies:
        copy.wait_recv()
    home_rows = m.mixed_home[...].reshape(2 * FRAMES, width)
    m.layer[...] = (
        f32(m.frames[...]) + dot(home_rows, m.w_out[...]).reshape(2, FRAMES, width)
    ).astype(bf16)
    stores.append(local(m.layer, layer_out, m.store.at[0]))

    early, sent = sent, []

    def pass_on(s, axis, block, kind):
        copies = []
        for step in (2, 1, 3):
            copies.append(
                send(
                    m.full.at[block],
                    m.full.at[block],
                    m.gs.at[s, NZ - 1 + kind * 3 + step - 1],
                    m.gr.at[s, NZ - 1 + kind * 3 + step - 1],
                    here.along(axis, step)[1],
                )
            )
        sent.extend(copies)
        return copies

    across, along = [], [{}, {}]
    for s in range(2):
        for copy in back[s]:
            copy.wait_recv()
        block, _ = third[s]
        across.append(pass_on(s, ORDERS[s][1], block, 0))
        along[s][0] = pass_on(s, ORDERS[s][0], block, 1)

    def sender(axis, step):
        return lax.rem(getattr(here, axis) + SIZES[axis] - step, SIZES[axis])

    for at, step in ((1, 1), (2, 3), (0, 2)):
        for s in range(2):
            axis, axis2, _ = ORDERS[s]
            across[s][at].wait_recv()
            block = (s, getattr(here, axis), sender(axis2, step))
            along[s][step] = pass_on(s, axis, block, 1 + step)
    block, part = tap_tile(here.z)
    m.tap_full[block, part] = tap_sum(tap_y, 8) * scale
    tap_back = []
    for step in far_first:
        tap_back.append(
            send(
                m.tap_full.at[block, part],
                m.tap_full.at[block, part],
                m.tgs.at[step - 1],
                m.tgr.at[step - 1],
                here.along("z", step)[1],
            )
        )
    sent += tap_back

    for copy in early:
        copy.wait_send()
    last = []
    for step in (0, 1, 3, 2):
        for s in range(2):
            for copy in along[s][step]:
                copy.wait_recv()
            index2 = sender(ORDERS[s][1], step)
            source = m.full.at[s, :, index2]
            target = grads_out.at[core, s, :, index2]
            stores.append(local(source, target, m.store.at[3 + s * 4 + step]))
            last.append(send(source, target, m.gcs.at[s, step], m.gcr.at[s, step], sibling))
    for copy in tap_back:
        copy.wait_recv()
    for block in range(4):
        m.tap_sum[:, block * 128 : (block + 1) * 128] = m.tap_full[block, 0:31]
    stores.append(local(m.tap_sum, tap_out, m.store.at[2]))
    for copy in sent:
        copy.wait_send()
    for copy in stores:
        copy.wait()
    for copy in last:
        copy.wait_send()
        copy.wait_recv()


def memory(width):
    bf16, full = jnp.bfloat16, jnp.float32
    dma = pltpu.SemaphoreType.DMA
    rows = (8, SHARE, width)
    home = (2, FRAMES, width)
    wide = (2, 4, FRAMES + 32, 128)
    square = pltpu.VMEM((width, width), bf16)
    return dict(
        frames=pltpu.VMEM(home, bf16),
        cot=pltpu.VMEM(home, bf16),
        taps=pltpu.VMEM((31, width), full),
        w_query=square,
        w_key=square,
        w_value=square,
        w_out=square,
        layer=pltpu.VMEM(home, bf16),
        fgrad=pltpu.VMEM(home, bf16),
        tap_sum=pltpu.VMEM((31, width), full),
        halo=pltpu.VMEM((2, 2, 16, width), bf16),
        ghalo=pltpu.VMEM((2, 2, 16, width), bf16),
        ends=pltpu.VMEM((2, 2, 16, width), bf16),
        pool=pltpu.VMEM((10,) + rows, bf16),
        acted=pltpu.VMEM(home, bf16),
        taps4=pltpu.VMEM((4, 32, 128), full),
        fpad=pltpu.VMEM(wide, full),
        gpad=pltpu.VMEM(wide, full),
        dsilu=pltpu.VMEM((2, 4, FRAMES, 128), full),
        gather_heads=pltpu.VMEM((width, 128), bf16),
        spread_heads=pltpu.VMEM((128, width), bf16),
        queries=pltpu.VMEM(rows, bf16),
        keys=pltpu.VMEM(rows, bf16),
        values=pltpu.VMEM(rows, bf16),
        ups=pltpu.VMEM(rows, bf16),
        dkey=pltpu.VMEM(rows, full),
        dvalue=pltpu.VMEM(rows, full),
        dacted=pltpu.VMEM(rows, bf16),
        dacted_home=pltpu.VMEM(home, bf16),
        mixed_home=pltpu.VMEM(home, bf16),
        mine=pltpu.VMEM((2, 4, 4, SECOND, 128), bf16),
        full=pltpu.VMEM((2, 4, 4, SECOND, 128), bf16),
        rx1=pltpu.VMEM((2, 3, 4, SECOND, 128), bf16),
        rx2=pltpu.VMEM((2, 3, SECOND, 128), bf16),
        rx3=pltpu.VMEM((2, NZ - 1, TILE, 128), bf16),
        tap0=pltpu.VMEM((4, 32, 128), full),
        tap_zrx=pltpu.VMEM((NZ - 1, 16, 128), full),
        tap_rx=pltpu.VMEM((12, 16, 128), full),
        tap_full=pltpu.VMEM((4, 32, 128), full),
        load=dma((7,)),
        store=dma((11,)),
        hs=dma((4,)),
        hr=dma((4,)),
        cs=dma((3,)),
        cr=dma((3,)),
        acs=dma((2, 3)),
        acr=dma((2, 3)),
        bs=dma((2, 3)),
        br=dma((2, 3)),
        core_s=dma((10,)),
        core_r=dma((10,)),
        s1=dma((2, 3, 4)),
        r1=dma((2, 3, 4)),
        s2=dma((2, 3)),
        r2=dma((2, 3)),
        s3=dma((2, NZ - 1)),
        r3=dma((2, NZ - 1)),
        gs=dma((2, NZ + 14)),
        gr=dma((2, NZ + 14)),
        gcs=dma((2, 4)),
        gcr=dma((2, 4)),
        ts=dma((NZ + 9,)),
        tr=dma((NZ + 9,)),
        tgs=dma((NZ - 1,)),
        tgr=dma((NZ - 1,)),
    )


def finish_body(layer, fgrad, taps, grads, layer_out, frame_grad, tap_out, *rest):
    outs, (packed, whole, held, held_taps, load, store) = rest[:4], rest[4:]
    chunks = [(g, half) for g in range(4) for half in range(2)]
    loads = []
    for at, (g, half) in enumerate(chunks):
        part = grads.at[g // 2, g % 2, :, pl.ds(half * 2, 2)]
        loads.append(local(part, packed.at[g, half], load.at[at]))
    small = ((layer, held.at[0], layer_out), (fgrad, held.at[1], frame_grad))
    small += ((taps, held_taps, tap_out),)
    first = [local(src, via, load.at[8 + at]) for at, (src, via, _) in enumerate(small)]
    moved = []
    for at, (g, half) in enumerate(chunks):
        loads[at].wait()
        rows = pl.ds(half * 256, 256)
        for block in range(4):
            value = f32(packed[g, half, block]).reshape(256, 128)
            whole[g, rows, block * 128 : (block + 1) * 128] = value
        moved.append(local(whole.at[g, rows], outs[g].at[rows], store.at[at]))
    for at, (_, via, dst) in enumerate(small):
        first[at].wait()
        moved.append(local(via, dst, store.at[8 + at]))
    for copy in moved:
        copy.wait()


def shards(frames, cotangent, kernel, w_query, w_key, w_value, w_out):
    number, length, width = frames.shape
    scale = 1.0 / math.sqrt(lax.axis_size("mic") * number * lax.axis_size("tm") * length)
    scratch = memory(width)
    bf16, full = jnp.bfloat16, jnp.float32
    shape = jax.ShapeDtypeStruct
    outputs = (shape(frames.shape, bf16), shape(frames.shape, bf16), shape(kernel.shape, full))

    def body(*refs):
        parts = types.SimpleNamespace(**dict(zip(scratch, refs[11:])))
        kernel_body(scale, *refs[:11], parts)

    parts = pl.pallas_call(
        body,
        out_shape=outputs + (shape((2, 2, 4, 4, SECOND, 128), bf16),),
        in_specs=[pl.BlockSpec(memory_space=pl.ANY)] * 7,
        out_specs=[pl.BlockSpec(memory_space=pl.ANY)] * 4,
        scratch_shapes=list(scratch.values()),
        compiler_params=pltpu.CompilerParams(
            collective_id=0, has_side_effects=True, vmem_limit_bytes=56 * 2**20
        ),
    )(frames, cotangent, kernel, w_query, w_key, w_value, w_out)
    dma = pltpu.SemaphoreType.DMA
    return pl.pallas_call(
        finish_body,
        out_shape=outputs + (shape((width, width), full),) * 4,
        in_specs=[pl.BlockSpec(memory_space=pl.ANY)] * 4,
        out_specs=[pl.BlockSpec(memory_space=pl.ANY)] * 7,
        scratch_shapes=[
            pltpu.VMEM((4, 2, 4, 2, SECOND, 128), bf16),
            pltpu.VMEM((4, width, width), full),
            pltpu.VMEM((2,) + frames.shape, bf16),
            pltpu.VMEM(kernel.shape, full),
            dma((11,)),
            dma((11,)),
        ],
        compiler_params=pltpu.CompilerParams(vmem_limit_bytes=56 * 2**20),
    )(*parts)


def solution(mesh):
    in_specs = (P("mic", "tm", None), P("mic", "tm", None), P(), P(), P(), P(), P())
    out_specs = (P("mic", "tm", None), P("mic", "tm", None), P(), P(), P(), P(), P())
    return jax.shard_map(shards, mesh=mesh, in_specs=in_specs, out_specs=out_specs, check_vma=False)
```

```python
import math
import types

import jax
import jax.numpy as jnp
from jax import lax
from jax.experimental import pallas as pl
from jax.experimental.pallas import tpu as pltpu
from jax.sharding import PartitionSpec as P

HEADS = 8
FRAMES = 128
SHARE = 32
NX, NY, NZ = 4, 4, 8
MESH = pl.DeviceIdType.MESH


class Place:
    def __init__(self):
        mic = lax.axis_index("mic")
        tm = lax.axis_index("tm")
        self.mic, self.tm = mic, tm
        self.core = lax.rem(mic, 2)
        self.x = lax.rem(tm, NX)
        self.z = lax.rem(lax.div(tm, NX), NZ)
        self.y = lax.div(tm, NX * NZ) * 2 + lax.div(mic, 2)

    def device(self, x=None, y=None, z=None, core=None):
        x = self.x if x is None else x
        y = self.y if y is None else y
        z = self.z if z is None else z
        core = self.core if core is None else core
        mic = lax.rem(y, 2) * 2 + core
        tm = lax.div(y, 2) * (NX * NZ) + z * NX + x
        return (mic, tm)

    def along(self, axis, step):
        size = {"x": NX, "y": NY, "z": NZ, "core": 2}[axis]
        index = lax.rem(getattr(self, axis) + step, size)
        return index, self.device(**{axis: index})


def rows_at(start, count):
    return pl.ds(pl.multiple_of(start, count), count)


def send(src, dst, send_sem, recv_sem, device):
    copy = pltpu.make_async_remote_copy(
        src_ref=src,
        dst_ref=dst,
        send_sem=send_sem,
        recv_sem=recv_sem,
        device_id=device,
        device_id_type=MESH,
    )
    copy.start()
    return copy


def local(src, dst, sem):
    copy = pltpu.make_async_copy(src, dst, sem)
    copy.start()
    return copy


SIZES = {"x": NX, "y": NY, "z": NZ, "core": 2}
SECOND, TILE = 128, 16
ORDERS = (("x", "y", "z"), ("y", "x", "z"))


ACT, ACT_S, MIXED, DQUERY, DKEY, DVALUE, COT, COT_S, FIRST_S, SECOND_S = range(10)


def f32(value):
    return value.astype(jnp.float32)


def dot(left, right, left_dim=1, right_dim=0):
    return lax.dot_general(
        left, right, (((left_dim,), (right_dim,)), ((), ())), preferred_element_type=jnp.float32
    )


def lanes(block):
    return pl.ds(pl.multiple_of(block * 128, 128), 128)


def shifted(padded, mic, block, base, count):
    for offset in range(1, 32):
        yield offset, padded[mic, block, base + offset : base + offset + count]


def kernel_body(
    scale,
    frames,
    cotangent,
    taps,
    w_query,
    w_key,
    w_value,
    w_out,
    layer_out,
    frame_grad,
    tap_out,
    grads_out,
    m,
):
    bf16 = jnp.bfloat16
    here = Place()
    width = frames.shape[2]
    rows = 8 * SHARE
    count = NX * NY * NZ // 2
    group = [lax.rem(here.mic + step, 4) for step in range(1, 4)]
    after = (here.mic, lax.rem(here.tm + 1, count))
    before = (here.mic, lax.rem(here.tm + count - 1, count))
    peers = [after, before]
    peers += [(mic, here.tm) for mic in group]
    for axis in ("core", "x", "y", "z"):
        for step in range(1, SIZES[axis]):
            peers.append(here.along(axis, step)[1])
    over = [lax.rem(here.x + step, NX) for step in range(1, NX)]
    peers += [here.device(x=x, core=1 - here.core) for x in over]
    barrier = pltpu.get_barrier_semaphore()
    for peer in peers:
        pl.semaphore_signal(barrier, inc=1, device_id=peer, device_id_type=MESH)
    loads = {}
    for at, (name, source) in enumerate(
        (
            ("frames", frames),
            ("taps", taps),
            ("cot", cotangent),
            ("w_out", w_out),
            ("w_query", w_query),
            ("w_key", w_key),
            ("w_value", w_value),
        )
    ):
        loads[name] = local(source, getattr(m, name), m.load.at[at])
    pl.semaphore_wait(barrier, len(peers))
    sent = []

    halo = [
        send(frames.at[:, pl.ds(FRAMES - 16, 16), :], m.halo.at[0], m.hs.at[0], m.hr.at[0], after),
        send(frames.at[:, pl.ds(0, 16), :], m.halo.at[1], m.hs.at[1], m.hr.at[1], before),
    ]
    mics_here = pl.ds(here.mic * 2, 2)
    share_here = rows_at(here.mic * SHARE, SHARE)
    cot_copies = []
    for step, mic in enumerate(group):
        cot_copies.append(
            send(
                cotangent.at[:, rows_at(mic * SHARE, SHARE), :],
                m.pool.at[COT, mics_here],
                m.cs.at[step],
                m.cr.at[step],
                (mic, here.tm),
            )
        )
    sent += halo + cot_copies
    loads["frames"].wait()
    loads["taps"].wait()
    for block in range(4):
        m.taps4[block, 0:31] = m.taps[:, block * 128 : (block + 1) * 128]
        for mic in range(2):
            m.fpad[mic, block, 16 : 16 + FRAMES] = f32(
                m.frames[mic, :, block * 128 : (block + 1) * 128]
            )

    def conv_rows(mic, block, base, number):
        conv = jnp.zeros((number, 128), jnp.float32)
        for offset, part in shifted(m.fpad, mic, block, base, number):
            conv = conv + part * m.taps4[block, offset - 1 : offset]
        sig = 1.0 / (1.0 + jnp.exp(-conv))
        m.acted[mic, base : base + number, lanes(block)] = (conv * sig).astype(bf16)
        m.dsilu[mic, block, base : base + number] = sig * (1.0 + conv * (1.0 - sig))

    def inner_block(step, carry):
        conv_rows(lax.div(step, 4), lax.rem(step, 4), 16, FRAMES - 32)
        return carry

    lax.fori_loop(0, 8, inner_block, 0)

    row = lax.broadcasted_iota(jnp.int32, (512, 128), 0)
    col = lax.broadcasted_iota(jnp.int32, (512, 128), 1)
    m.gather_heads[...] = jnp.where(lax.div(row, 64) == col, 1.0, 0.0).astype(bf16)
    row = lax.broadcasted_iota(jnp.int32, (128, 512), 0)
    col = lax.broadcasted_iota(jnp.int32, (128, 512), 1)
    m.spread_heads[...] = jnp.where(lax.div(col, 64) == row, 1.0, 0.0).astype(bf16)
    loads["cot"].wait()
    m.pool[COT, mics_here] = m.cot[:, share_here, :]

    def fill_halo(side, pad, buffer, copy):
        copy.wait_recv()
        inside = here.tm > 0 if side == 0 else here.tm < count - 1
        place = slice(0, 16) if side == 0 else slice(16 + FRAMES, 32 + FRAMES)
        for mic in range(2):
            for block in range(4):
                value = f32(buffer[side, mic, :, block * 128 : (block + 1) * 128])
                pad[mic, block, place] = jnp.where(inside, value, 0.0)

    for side in range(2):
        fill_halo(side, m.fpad, m.halo, halo[side])

    act_copies = []
    for mic in range(2):

        def outer_block(block, carry):
            conv_rows(mic, block, 0, 16)
            conv_rows(mic, block, FRAMES - 16, 16)
            return carry

        lax.fori_loop(0, 4, outer_block, 0)
        for step, target in enumerate(group):
            act_copies.append(
                send(
                    m.acted.at[mic, rows_at(target * SHARE, SHARE), :],
                    m.pool.at[ACT, here.mic * 2 + mic],
                    m.acs.at[mic, step],
                    m.acr.at[mic, step],
                    (target, here.tm),
                )
            )
        m.pool[ACT, here.mic * 2 + mic] = m.acted[mic, share_here, :]
    sent += act_copies

    other, sibling = here.along("core", 1)

    def to_sibling(source, target):
        copy = send(
            m.pool.at[source],
            m.pool.at[target],
            m.core_s.at[target],
            m.core_r.at[target],
            sibling,
        )
        sent.append(copy)
        return copy

    for copy in cot_copies:
        copy.wait_recv()
    shared = {COT_S: to_sibling(COT, COT_S)}
    cot_rows = m.pool[COT].reshape(rows, width)
    loads["w_out"].wait()
    m.ups[...] = dot(cot_rows, m.w_out[...], 1, 1).astype(bf16).reshape(8, SHARE, width)
    for name in ("w_query", "w_key", "w_value"):
        loads[name].wait()
    for copy in act_copies:
        copy.wait_recv()
    shared[ACT_S] = to_sibling(ACT, ACT_S)
    act_rows = m.pool[ACT].reshape(rows, width)
    for weight, target in ((m.w_query, m.queries), (m.w_key, m.keys), (m.w_value, m.values)):
        target[...] = dot(act_rows, weight[...]).astype(bf16).reshape(8, SHARE, width)

    factor = 1.0 / math.sqrt(width // HEADS)

    def attend(index):
        query, up = m.queries[index], m.ups[index]
        keys, values = m.keys[...], m.values[...]
        gather, spread = m.gather_heads[...], m.spread_heads[...]

        def per_head(product):
            return dot(product.reshape(rows, width), gather).reshape(8, SHARE, 128)

        def per_lane(heads):
            return dot(heads.astype(bf16).reshape(rows, 128), spread).reshape(8, SHARE, width)

        weights = jnp.exp(per_head(query[None] * keys) * factor)
        weights = weights / jnp.sum(weights, axis=0, keepdims=True)
        products = per_head(up[None] * values)
        inner = weights * (products - jnp.sum(weights * products, axis=0, keepdims=True)) * factor
        weights, inner = per_lane(weights), per_lane(inner)
        m.pool[MIXED, index] = jnp.sum(weights * f32(values), axis=0).astype(bf16)
        m.pool[DQUERY, index] = jnp.sum(inner * f32(keys), axis=0).astype(bf16)
        return inner * f32(query)[None], weights * f32(up)[None]

    def attend_four(step, carry):
        dkey, dvalue = attend(4 * step)
        for index in range(1, 4):
            dkey_too, dvalue_too = attend(4 * step + index)
            dkey, dvalue = dkey + dkey_too, dvalue + dvalue_too

        @pl.when(step == 0)
        def _():
            m.dkey[...] = dkey
            m.dvalue[...] = dvalue

        @pl.when(step > 0)
        def _():
            m.dkey[...] += dkey
            m.dvalue[...] += dvalue

        return carry

    lax.fori_loop(0, 2, attend_four, 0)

    shared[FIRST_S] = to_sibling(DQUERY - other, FIRST_S)
    m.pool[DKEY] = m.dkey[...].astype(bf16)
    m.pool[DVALUE] = m.dvalue[...].astype(bf16)
    shared[SECOND_S] = to_sibling(DKEY + other, SECOND_S)

    def pooled(index):
        return m.pool[index].reshape(rows, width)

    dacted = dot(pooled(DQUERY), m.w_query[...], 1, 1)
    dacted = dacted + dot(pooled(DKEY), m.w_key[...], 1, 1)
    dacted = dacted + dot(pooled(DVALUE), m.w_value[...], 1, 1)
    m.dacted[...] = dacted.astype(bf16).reshape(8, SHARE, width)
    def send_home(kind, source, target):
        copies = []
        for step, mic in enumerate(group):
            copies.append(
                send(
                    source.at[pl.ds(mic * 2, 2)],
                    target.at[:, share_here, :],
                    m.bs.at[kind, step],
                    m.br.at[kind, step],
                    (mic, here.tm),
                )
            )
        target[:, share_here, :] = source[mics_here]
        sent.extend(copies)
        return copies

    dacted_copies = send_home(0, m.dacted, m.dacted_home)

    core = here.core
    operands = (
        ((ACT, DQUERY + 2 * core), (ACT_S, FIRST_S + core)),
        ((2 * core, DKEY + 2 * core), (ACT_S + 7 * core, SECOND_S - 2 * core)),
    )
    terms = []
    for mine, _ in operands:
        terms.append(dot(pooled(mine[0]), pooled(mine[1]), 0, 0))
    for copy in shared.values():
        copy.wait_recv()
    first = [{}, {}]
    for s in range(2):
        _, theirs = operands[s]
        term = (terms[s] + dot(pooled(theirs[0]), pooled(theirs[1]), 0, 0)).astype(bf16)
        for block in range(4):
            m.mine[s, block] = term[:, block * 128 : (block + 1) * 128].reshape(4, SECOND, 128)
        axis, axis2, _ = ORDERS[s]
        for far in (2, 1, 3, 0):
            index2, _ = here.along(axis2, far)
            for step in (2, 1, 3):
                index, peer = here.along(axis, step)
                first[s][far, step] = send(
                    m.mine.at[s, index, index2],
                    m.rx1.at[s, step - 1, far],
                    m.s1.at[s, step - 1, far],
                    m.r1.at[s, step - 1, far],
                    peer,
                )
        sent += first[s].values()

    for copy in dacted_copies:
        copy.wait_recv()

    def dconv_block(step, carry):
        mic, block = lax.div(step, 4), lax.rem(step, 4)
        dconv = f32(m.dacted_home[mic, :, lanes(block)]) * m.dsilu[mic, block]
        m.gpad[mic, block, 16 : 16 + FRAMES] = dconv
        m.ends[0, mic, :, lanes(block)] = dconv[FRAMES - 16 :].astype(bf16)
        m.ends[1, mic, :, lanes(block)] = dconv[:16].astype(bf16)
        return carry

    lax.fori_loop(0, 8, dconv_block, 0)
    ghalo = [
        send(m.ends.at[0], m.ghalo.at[0], m.hs.at[2], m.hr.at[2], after),
        send(m.ends.at[1], m.ghalo.at[1], m.hs.at[3], m.hr.at[3], before),
    ]
    sent += ghalo

    def tap_block(block, carry):
        sums = {}
        for mic in range(2):
            dconv = m.gpad[mic, block, 16 : 16 + FRAMES]
            for offset, part in shifted(m.fpad, mic, block, 0, FRAMES):
                part = jnp.sum((part * dconv).reshape(FRAMES // 8, 8, 128), axis=0)
                sums[offset] = sums[offset] + part if mic else part
        for offset, part in sums.items():
            m.tap0[block, offset - 1 : offset] = jnp.sum(part, axis=0, keepdims=True)
        m.tap0[block, 31:32] = jnp.zeros((1, 128), jnp.float32)
        return carry

    lax.fori_loop(0, 4, tap_block, 0)

    def tap_tile(index):
        return lax.div(index, 2), rows_at(lax.rem(index, 2) * 16, 16)

    tap_copies = []
    for step in range(1, NZ):
        index, peer = here.along("z", step)
        block, part = tap_tile(index)
        tap_copies.append(
            send(
                m.tap0.at[block, part],
                m.tap_zrx.at[step - 1],
                m.ts.at[step - 1],
                m.tr.at[step - 1],
                peer,
            )
        )
    sent += tap_copies

    second = [{}, {}]
    for far in (2, 1, 3, 0):
        for s in range(2):
            axis, axis2, _ = ORDERS[s]
            index = getattr(here, axis)
            index2, peer = here.along(axis2, far)
            total = f32(m.mine[s, index, index2])
            for step in (1, 2, 3):
                first[s][far, step].wait_recv()
                total = total + f32(m.rx1[s, step - 1, far])
            m.mine[s, index, index2] = total.astype(bf16)
            if far:
                second[s][far] = send(
                    m.mine.at[s, index, index2],
                    m.rx2.at[s, far - 1],
                    m.s2.at[s, far - 1],
                    m.r2.at[s, far - 1],
                    peer,
                )
                sent.append(second[s][far])

    far_first = (4, 3, 5, 2, 6, 1, 7)
    third = []
    for s in range(2):
        axis, axis2, _ = ORDERS[s]
        block = (s, getattr(here, axis), getattr(here, axis2))
        total = f32(m.mine[block])
        for far in (1, 2, 3):
            second[s][far].wait_recv()
            total = total + f32(m.rx2[s, far - 1])
        m.mine[block] = total.astype(bf16)
        copies = []
        for step in far_first:
            index, peer = here.along("z", step)
            copies.append(
                send(
                    m.mine.at[block + (rows_at(index * TILE, TILE),)],
                    m.rx3.at[s, step - 1],
                    m.s3.at[s, step - 1],
                    m.r3.at[s, step - 1],
                    peer,
                )
            )
        third.append((block, copies))
        sent += copies
    mixed_copies = send_home(1, m.pool.at[MIXED], m.mixed_home)

    for side in range(2):
        fill_halo(side, m.gpad, m.ghalo, ghalo[side])

    def grad_block(step, carry):
        mic, block = lax.div(step, 4), lax.rem(step, 4)
        total = f32(m.cot[mic, :, lanes(block)])
        for offset, part in shifted(m.gpad, mic, block, 0, FRAMES):
            total = total + part * m.taps4[block, 31 - offset : 32 - offset]
        m.fgrad[mic, :, lanes(block)] = total.astype(bf16)
        return carry

    lax.fori_loop(0, 8, grad_block, 0)
    stores = [local(m.fgrad, frame_grad, m.store.at[1])]

    block, part = tap_tile(here.z)
    total = m.tap0[block, part]
    for step in range(1, NZ):
        tap_copies[step - 1].wait_recv()
        total = total + m.tap_zrx[step - 1]

    def tap_share(tile, slot, base, others):
        m.tap_rx[slot] = tile
        copies = []
        for at, peer in enumerate(others):
            copies.append(
                send(m.tap_rx.at[slot], m.tap_rx.at[slot], m.ts.at[base + at], m.tr.at[base + at], peer)
            )
        return copies

    def tap_sum(copies, base):
        for copy in copies:
            copy.wait_recv()
        total = m.tap_rx[base]
        for index in range(len(copies)):
            total = total + m.tap_rx[base + 1 + index]
        return total

    others = [here.device(x=x, core=core) for x in over for core in (here.core, 1 - here.core)]
    others.append(sibling)
    tap_x = tap_share(total, here.x * 2 + here.core, NZ - 1, others)
    sent += tap_x

    back = []
    for s in range(2):
        block, copies = third[s]
        part = block + (rows_at(here.z * TILE, TILE),)
        total = f32(m.mine[part])
        for copy in copies:
            copy.wait_recv()
        for step in range(NZ - 1):
            total = total + f32(m.rx3[s, step])
        m.full[part] = (total * scale).astype(bf16)
        copies = []
        for step in far_first:
            copies.append(
                send(
                    m.full.at[part],
                    m.full.at[part],
                    m.gs.at[s, step - 1],
                    m.gr.at[s, step - 1],
                    here.along("z", step)[1],
                )
            )
        back.append(copies)
        sent += copies

    others = [here.along("y", step)[1] for step in (2, 1, 3)]
    tap_y = tap_share(tap_sum(tap_x, 0), 8 + here.y, NZ + 6, others)
    sent += tap_y

    for copy in mixed_copies:
        copy.wait_recv()
    home_rows = m.mixed_home[...].reshape(2 * FRAMES, width)
    m.layer[...] = (
        f32(m.frames[...]) + dot(home_rows, m.w_out[...]).reshape(2, FRAMES, width)
    ).astype(bf16)
    stores.append(local(m.layer, layer_out, m.store.at[0]))

    early, sent = sent, []

    def pass_on(s, axis, block, kind):
        copies = []
        for step in (2, 1, 3):
            copies.append(
                send(
                    m.full.at[block],
                    m.full.at[block],
                    m.gs.at[s, NZ - 1 + kind * 3 + step - 1],
                    m.gr.at[s, NZ - 1 + kind * 3 + step - 1],
                    here.along(axis, step)[1],
                )
            )
        sent.extend(copies)
        return copies

    across, along = [], [{}, {}]
    for s in range(2):
        for copy in back[s]:
            copy.wait_recv()
        block, _ = third[s]
        across.append(pass_on(s, ORDERS[s][1], block, 0))
        along[s][0] = pass_on(s, ORDERS[s][0], block, 1)

    def sender(axis, step):
        return lax.rem(getattr(here, axis) + SIZES[axis] - step, SIZES[axis])

    for at, step in ((1, 1), (2, 3), (0, 2)):
        for s in range(2):
            axis, axis2, _ = ORDERS[s]
            across[s][at].wait_recv()
            block = (s, getattr(here, axis), sender(axis2, step))
            along[s][step] = pass_on(s, axis, block, 1 + step)
    block, part = tap_tile(here.z)
    m.tap_full[block, part] = tap_sum(tap_y, 8) * scale
    tap_back = []
    for step in far_first:
        tap_back.append(
            send(
                m.tap_full.at[block, part],
                m.tap_full.at[block, part],
                m.tgs.at[step - 1],
                m.tgr.at[step - 1],
                here.along("z", step)[1],
            )
        )
    sent += tap_back

    for copy in early:
        copy.wait_send()
    last = []
    for step in (0, 1, 3, 2):
        for s in range(2):
            for copy in along[s][step]:
                copy.wait_recv()
            index2 = sender(ORDERS[s][1], step)
            source = m.full.at[s, :, index2]
            target = grads_out.at[core, s, :, index2]
            stores.append(local(source, target, m.store.at[3 + s * 4 + step]))
            last.append(send(source, target, m.gcs.at[s, step], m.gcr.at[s, step], sibling))
    for copy in tap_back:
        copy.wait_recv()
    for block in range(4):
        m.tap_sum[:, block * 128 : (block + 1) * 128] = m.tap_full[block, 0:31]
    stores.append(local(m.tap_sum, tap_out, m.store.at[2]))
    for copy in sent:
        copy.wait_send()
    for copy in stores:
        copy.wait()
    for copy in last:
        copy.wait_send()
        copy.wait_recv()


def memory(width):
    bf16, full = jnp.bfloat16, jnp.float32
    dma = pltpu.SemaphoreType.DMA
    rows = (8, SHARE, width)
    home = (2, FRAMES, width)
    wide = (2, 4, FRAMES + 32, 128)
    square = pltpu.VMEM((width, width), bf16)
    return dict(
        frames=pltpu.VMEM(home, bf16),
        cot=pltpu.VMEM(home, bf16),
        taps=pltpu.VMEM((31, width), full),
        w_query=square,
        w_key=square,
        w_value=square,
        w_out=square,
        layer=pltpu.VMEM(home, bf16),
        fgrad=pltpu.VMEM(home, bf16),
        tap_sum=pltpu.VMEM((31, width), full),
        halo=pltpu.VMEM((2, 2, 16, width), bf16),
        ghalo=pltpu.VMEM((2, 2, 16, width), bf16),
        ends=pltpu.VMEM((2, 2, 16, width), bf16),
        pool=pltpu.VMEM((10,) + rows, bf16),
        acted=pltpu.VMEM(home, bf16),
        taps4=pltpu.VMEM((4, 32, 128), full),
        fpad=pltpu.VMEM(wide, full),
        gpad=pltpu.VMEM(wide, full),
        dsilu=pltpu.VMEM((2, 4, FRAMES, 128), full),
        gather_heads=pltpu.VMEM((width, 128), bf16),
        spread_heads=pltpu.VMEM((128, width), bf16),
        queries=pltpu.VMEM(rows, bf16),
        keys=pltpu.VMEM(rows, bf16),
        values=pltpu.VMEM(rows, bf16),
        ups=pltpu.VMEM(rows, bf16),
        dkey=pltpu.VMEM(rows, full),
        dvalue=pltpu.VMEM(rows, full),
        dacted=pltpu.VMEM(rows, bf16),
        dacted_home=pltpu.VMEM(home, bf16),
        mixed_home=pltpu.VMEM(home, bf16),
        mine=pltpu.VMEM((2, 4, 4, SECOND, 128), bf16),
        full=pltpu.VMEM((2, 4, 4, SECOND, 128), bf16),
        rx1=pltpu.VMEM((2, 3, 4, SECOND, 128), bf16),
        rx2=pltpu.VMEM((2, 3, SECOND, 128), bf16),
        rx3=pltpu.VMEM((2, NZ - 1, TILE, 128), bf16),
        tap0=pltpu.VMEM((4, 32, 128), full),
        tap_zrx=pltpu.VMEM((NZ - 1, 16, 128), full),
        tap_rx=pltpu.VMEM((12, 16, 128), full),
        tap_full=pltpu.VMEM((4, 32, 128), full),
        load=dma((7,)),
        store=dma((11,)),
        hs=dma((4,)),
        hr=dma((4,)),
        cs=dma((3,)),
        cr=dma((3,)),
        acs=dma((2, 3)),
        acr=dma((2, 3)),
        bs=dma((2, 3)),
        br=dma((2, 3)),
        core_s=dma((10,)),
        core_r=dma((10,)),
        s1=dma((2, 3, 4)),
        r1=dma((2, 3, 4)),
        s2=dma((2, 3)),
        r2=dma((2, 3)),
        s3=dma((2, NZ - 1)),
        r3=dma((2, NZ - 1)),
        gs=dma((2, NZ + 14)),
        gr=dma((2, NZ + 14)),
        gcs=dma((2, 4)),
        gcr=dma((2, 4)),
        ts=dma((NZ + 9,)),
        tr=dma((NZ + 9,)),
        tgs=dma((NZ - 1,)),
        tgr=dma((NZ - 1,)),
    )


def finish_body(layer, fgrad, taps, grads, layer_out, frame_grad, tap_out, *rest):
    outs, (packed, whole, held, held_taps, load, store) = rest[:4], rest[4:]
    chunks = [(g, half) for g in range(4) for half in range(2)]
    loads = []
    for at, (g, half) in enumerate(chunks):
        part = grads.at[g // 2, g % 2, :, pl.ds(half * 2, 2)]
        loads.append(local(part, packed.at[g, half], load.at[at]))
    small = ((layer, held.at[0], layer_out), (fgrad, held.at[1], frame_grad))
    small += ((taps, held_taps, tap_out),)
    first = [local(src, via, load.at[8 + at]) for at, (src, via, _) in enumerate(small)]
    moved = []
    for at, (g, half) in enumerate(chunks):
        loads[at].wait()
        rows = pl.ds(half * 256, 256)
        for block in range(4):
            value = f32(packed[g, half, block]).reshape(256, 128)
            whole[g, rows, block * 128 : (block + 1) * 128] = value
        moved.append(local(whole.at[g, rows], outs[g].at[rows], store.at[at]))
    for at, (_, via, dst) in enumerate(small):
        first[at].wait()
        moved.append(local(via, dst, store.at[8 + at]))
    for copy in moved:
        copy.wait()


def shards(frames, cotangent, kernel, w_query, w_key, w_value, w_out):
    number, length, width = frames.shape
    scale = 1.0 / math.sqrt(lax.axis_size("mic") * number * lax.axis_size("tm") * length)
    scratch = memory(width)
    bf16, full = jnp.bfloat16, jnp.float32
    shape = jax.ShapeDtypeStruct
    outputs = (shape(frames.shape, bf16), shape(frames.shape, bf16), shape(kernel.shape, full))

    def body(*refs):
        parts = types.SimpleNamespace(**dict(zip(scratch, refs[11:])))
        kernel_body(scale, *refs[:11], parts)

    parts = pl.pallas_call(
        body,
        out_shape=outputs + (shape((2, 2, 4, 4, SECOND, 128), bf16),),
        in_specs=[pl.BlockSpec(memory_space=pl.ANY)] * 7,
        out_specs=[pl.BlockSpec(memory_space=pl.ANY)] * 4,
        scratch_shapes=list(scratch.values()),
        compiler_params=pltpu.CompilerParams(
            collective_id=0, has_side_effects=True, vmem_limit_bytes=56 * 2**20
        ),
    )(frames, cotangent, kernel, w_query, w_key, w_value, w_out)
    dma = pltpu.SemaphoreType.DMA
    return pl.pallas_call(
        finish_body,
        out_shape=outputs + (shape((width, width), full),) * 4,
        in_specs=[pl.BlockSpec(memory_space=pl.ANY)] * 4,
        out_specs=[pl.BlockSpec(memory_space=pl.ANY)] * 7,
        scratch_shapes=[
            pltpu.VMEM((4, 2, 4, 2, SECOND, 128), bf16),
            pltpu.VMEM((4, width, width), full),
            pltpu.VMEM((2,) + frames.shape, bf16),
            pltpu.VMEM(kernel.shape, full),
            dma((11,)),
            dma((11,)),
        ],
        compiler_params=pltpu.CompilerParams(vmem_limit_bytes=56 * 2**20),
    )(*parts)


def solution(mesh):
    in_specs = (P("mic", "tm", None), P("mic", "tm", None), P(), P(), P(), P(), P())
    out_specs = (P("mic", "tm", None), P("mic", "tm", None), P(), P(), P(), P(), P())
    return jax.shard_map(shards, mesh=mesh, in_specs=in_specs, out_specs=out_specs, check_vma=False)
```
